512 devices in a mesh: ctx: 64 (over y_lo, z, core), head: 8 (over y_hi, x).
Axes of the slice: x: 4, y: 8 (y_hi: 2, y_lo: 4; y = y_hi * 4 + y_lo), z: 8, core: 2. Of those that a mesh axis runs over, the one named last changes fastest.
Arguments:
- streams: bfloat16 [8192, 8, 1024], P(('ctx', 'head'))
- steps: bfloat16 [8192, 8, 4], P(('ctx', 'head')), may hold values from -1 to 2, as said below
- skip_d: float32 [16], P('head'), may hold values from 0.5 to 2
- ssm_gain: float32 [1024], P('head'), may hold values from 0.1 to 1.9
- w_out: bfloat16 [3072, 2560], P('head'), may hold values from -0.109375 to 0.109375
Outputs:
- mixed: bfloat16 [8192, 2560], P(('ctx', 'head'))
The draws below stay inside these ranges and needn't reach their ends.
Inputs may be any that keep to these rules, and one draw needn't show every extreme that they name: `steps`: the first 2 entries of a row are step sizes of 0.5 to 2; the last 2 are logarithms of decay factors, never positive.
All inputs are finite; a program needn't handle non-finite values.
Results may differ from the reference program's by a relative error of at most 0.017.
Values may be sent and summed in bfloat16 or wider, within the bound.
A program may use at most 64 MiB of HBM per device.

```python
import math
import jax
import jax.numpy as jnp
from jax import lax

HD = 128
HQ_DEV = 2
SH = 2
HP = 64
NST = 128
DOUT = 2560
TOK_CTX = 128
SEQUENCE_TOKENS = 8192
FEAT = 1024
WROWS = 384
N_CTX = 64
N_HEAD = 8


def draw_streams(key, part):
    key = jax.random.fold_in(key, 1)
    splits = jax.random.split(key, 11)
    key_base, key_dir, key_slant_weight, key_val = (splits[0], splits[1], splits[2], splits[3])
    key_pattern, key_marked, key_spot, key_choice = (splits[4], splits[5], splits[6], splits[7])
    key_aim, key_pick, key_low = (splits[8], splits[9], splits[10])
    normals = jax.random.normal(key_base, (SEQUENCE_TOKENS, N_HEAD, FEAT), jnp.float32)
    q_width = HQ_DEV * HD
    direction = 0.5 * jax.random.normal(key_dir, (N_HEAD, HD), jnp.float32)
    row_index_list = jnp.arange(SEQUENCE_TOKENS, dtype=jnp.int32)
    block_total = SEQUENCE_TOKENS // TOK_CTX
    block_ids = row_index_list // TOK_CTX
    inner = row_index_list % TOK_CTX
    half_rows = TOK_CTX // 2
    early = block_ids * half_rows + inner
    late = (2 * block_total - 1 - block_ids) * half_rows + inner - half_rows
    positions = jnp.where(inner < half_rows, early, late).astype(jnp.int32)
    num_blocks = SEQUENCE_TOKENS // 64
    pos_block = positions // 64
    marked = jax.random.randint(key_marked, (num_blocks, N_HEAD), 0, 2) == 1
    spot = jax.random.randint(key_spot, (num_blocks, N_HEAD), 0, 64)
    pattern_ids = jax.random.randint(key_choice, (num_blocks, N_HEAD), 0, 4)
    open_tilt = jax.random.uniform(key_slant_weight, (num_blocks, N_HEAD), jnp.float32, -1.5, 1.5)
    low_tilt = jax.random.uniform(key_low, (num_blocks, N_HEAD), jnp.float32, -1.5, -0.75)
    tilt_table = jnp.where(marked, low_tilt, open_tilt)
    tilted = tilt_table[pos_block]
    patterns = 1.4 * jax.random.normal(key_pattern, (N_HEAD, 4, HD), jnp.float32)
    head_ids = jnp.arange(N_HEAD, dtype=jnp.int32)
    needle = marked[pos_block] & ((positions % 64)[:, None] == spot[pos_block])
    key_extra = patterns[head_ids[None, :], pattern_ids[pos_block]]
    aim_on = jax.random.randint(key_aim, (SEQUENCE_TOKENS, N_HEAD, HQ_DEV), 0, 2) == 1
    aim_ids = jax.random.randint(key_pick, (SEQUENCE_TOKENS, N_HEAD, HQ_DEV), 0, 4)
    query_extra = patterns[head_ids[None, :, None], aim_ids]
    offsets = jnp.repeat(jax.random.normal(key_val, (num_blocks, N_HEAD, HD), jnp.float32), 64, axis=0)
    queries = normals[:, :, :q_width].reshape(SEQUENCE_TOKENS, N_HEAD, HQ_DEV, HD) + direction[None, :, None, :]
    queries = queries + jnp.where(aim_on[:, :, :, None], query_extra, 0.0)
    keys = normals[:, :, q_width:q_width + HD] + tilted[:, :, None] * direction[None, :, :]
    keys = keys + jnp.where(needle[:, :, None], key_extra, 0.0)
    values = normals[:, :, q_width + HD:q_width + 2 * HD] + offsets
    lead = q_width + 2 * HD
    gates = normals[:, :, lead:lead + 2 * SH * HP]
    b_and_c = normals[:, :, lead + 2 * SH * HP:] * NST ** (-0.5)
    joined = jnp.concatenate([queries.reshape(SEQUENCE_TOKENS, N_HEAD, q_width), keys, values, gates, b_and_c], axis=-1)
    return joined.astype(jnp.bfloat16)


def draw_steps(key, part):
    key = jax.random.fold_in(key, 2)
    key_dt, key_kind, key_fast, key_slow, key_rough, key_location_index, key_loss = jax.random.split(key, 7)
    heads = N_HEAD * SH
    step_size = jnp.exp(jax.random.uniform(key_dt, (SEQUENCE_TOKENS, heads), jnp.float32, math.log(0.5), math.log(2.0)))
    fast_limit = 8
    is_fast = jax.random.randint(key_kind, (heads,), 0, 16) < fast_limit
    fast_rate = jnp.exp(jax.random.uniform(key_fast, (heads,), jnp.float32, math.log(1.0 / 300.0), math.log(1.0 / 30.0)))
    slow_rate = jnp.exp(jax.random.uniform(key_slow, (heads,), jnp.float32, math.log(0.2), math.log(0.5))) / SEQUENCE_TOKENS
    rates = jnp.where(is_fast, fast_rate, slow_rate)
    rough = jax.random.uniform(key_rough, (SEQUENCE_TOKENS, heads), jnp.float32, 0.5, 2.0)
    log_decay = -rates[None, :] * rough
    gathered_row_span = jax.random.randint(key_location_index, (3,), 0, SEQUENCE_TOKENS)
    losses = jax.random.uniform(key_loss, (3, heads), jnp.float32, 0.22, 0.69)
    row_index_list = jnp.arange(SEQUENCE_TOKENS, dtype=jnp.int32)
    match_count = row_index_list[:, None] == gathered_row_span[None, :]
    log_decay = log_decay - jnp.sum(jnp.where(match_count[:, :, None], losses[None, :, :], 0.0), axis=1)
    joined = jnp.concatenate([step_size.reshape(SEQUENCE_TOKENS, N_HEAD, SH), log_decay.reshape(SEQUENCE_TOKENS, N_HEAD, SH)], axis=-1)
    return joined.astype(jnp.bfloat16)


def levels(stream_key, shape, cuts, least, high):
    def one(axis_at, parts):
        draws = jax.random.uniform(jax.random.fold_in(jax.random.fold_in(stream_key, 6), axis_at), (parts,), jnp.float32, least / len(cuts), high / len(cuts))
        return jnp.repeat(jnp.exp(draws), shape[axis_at] // parts).reshape((-1,) + (1,) * (len(shape) - axis_at - 1))

    gain = one(*cuts[0])
    for cut in cuts[1:]:
        gain = gain * one(*cut)
    return gain


def scatter_about(stream_key, shape, spread, bound, cuts=(), kind=jnp.bfloat16):
    values = jax.random.normal(stream_key, shape, jnp.float32) * spread
    if len(cuts) > 0:
        values = levels(stream_key, shape, cuts, -0.22, 0.18) * values
    return jnp.clip(values, min=-bound, max=bound).astype(kind)


def setup_inputs(seed: int = 0) -> dict:
    key_list = jax.random.split(jax.random.key(seed), 6)
    streams = draw_streams(jax.random.fold_in(key_list[5], 71), 0)
    steps = draw_steps(jax.random.fold_in(key_list[5], 71), 0)
    skip_d = jnp.clip(jnp.exp(math.log(2.0) - 1.3862944 * jax.random.uniform(key_list[2], (N_HEAD * SH,), jnp.float32) ** levels(key_list[2], (N_HEAD * SH,), ((0, 8),), -0.2, 0.2)), 0.5, 2.0)
    ssm_gain = jnp.clip(1.0 + 0.18 * jax.random.normal(key_list[3], (N_HEAD * SH * HP,), jnp.float32), 0.1, 1.9)
    w_out = scatter_about(key_list[4], (N_HEAD * WROWS, DOUT), (N_HEAD * WROWS) ** -0.5, 0.109375, ((0, 8),))
    return {"streams": streams, "steps": steps, "skip_d": skip_d, "ssm_gain": ssm_gain, "w_out": w_out}


def seq_positions():
    row_index_list = jnp.arange(SEQUENCE_TOKENS, dtype=jnp.int32)
    block_ids = row_index_list // TOK_CTX
    inner = row_index_list % TOK_CTX
    half_rows = TOK_CTX // 2
    early = block_ids * half_rows + inner
    late = (2 * N_CTX - 1 - block_ids) * half_rows + inner - half_rows
    return jnp.where(inner < half_rows, early, late).astype(jnp.int32)

def attend_group(operands):
    queries, keys, values = operands
    key_f = keys.astype(jnp.float32)
    value_f = values.astype(jnp.float32)
    key_pos = jnp.arange(SEQUENCE_TOKENS, dtype=jnp.int32)
    scale_factor = 1.0 / math.sqrt(HD)
    q_blocks = queries.reshape(SEQUENCE_TOKENS // 512, 512, HQ_DEV, HD)
    offsets = jnp.arange(SEQUENCE_TOKENS // 512, dtype=jnp.int32) * 512

    def one_block(paired):
        q_block, offset = paired
        scores = jnp.einsum('qhd,kd->hqk', q_block.astype(jnp.float32), key_f) * scale_factor
        q_pos = offset + jnp.arange(512, dtype=jnp.int32)
        visible = key_pos[None, None, :] <= q_pos[None, :, None]
        highest = lax.optimization_barrier(jnp.max(jnp.where(visible, scores, -jnp.inf), axis=-1, keepdims=True))
        probs = jnp.where(visible, jnp.exp(scores - highest), 0.0)
        totals = lax.optimization_barrier(jnp.sum(probs, axis=-1))
        rounded = lax.optimization_barrier(probs.astype(jnp.bfloat16)).astype(jnp.float32)
        weighted = jnp.einsum('hqk,kd->qhd', rounded, value_f)
        return (weighted / jnp.transpose(totals)[:, :, None]).astype(jnp.bfloat16)
    return lax.map(one_block, (q_blocks, offsets)).reshape(SEQUENCE_TOKENS, HQ_DEV, HD)

def reference(streams, steps, skip_d, ssm_gain, w_out):
    positions = seq_positions()
    order = jnp.zeros((SEQUENCE_TOKENS,), jnp.int32).at[positions].set(jnp.arange(SEQUENCE_TOKENS, dtype=jnp.int32))
    ordered = streams[order]
    step_vals = steps[order].astype(jnp.float32)
    q_width = HQ_DEV * HD
    queries = ordered[:, :, :q_width].reshape(SEQUENCE_TOKENS, N_HEAD, HQ_DEV, HD)
    keys = ordered[:, :, q_width:q_width + HD]
    values = ordered[:, :, q_width + HD:q_width + 2 * HD]
    lead = q_width + 2 * HD
    ssm_width = SH * HP
    ssm_in = ordered[:, :, lead:lead + ssm_width].astype(jnp.float32).reshape(SEQUENCE_TOKENS, N_HEAD, SH, HP)
    gate_z = ordered[:, :, lead + ssm_width:lead + 2 * ssm_width].astype(jnp.float32)
    b_proj = ordered[:, :, lead + 2 * ssm_width:lead + 2 * ssm_width + NST].astype(jnp.float32)
    c_proj = ordered[:, :, lead + 2 * ssm_width + NST:].astype(jnp.float32)
    attn = lax.map(attend_group, (jnp.moveaxis(queries, 1, 0), jnp.moveaxis(keys, 1, 0), jnp.moveaxis(values, 1, 0)))
    attn = jnp.moveaxis(attn, 0, 1).reshape(SEQUENCE_TOKENS, N_HEAD, q_width)
    step_size = step_vals[:, :, :SH]
    decays = jnp.exp(step_vals[:, :, SH:])

    def advance(stored, layer_input_rows):
        decay_t, size_t, in_t, b_t, c_t = layer_input_rows
        stored = decay_t[:, :, None, None] * stored + (size_t[:, :, None] * in_t)[:, :, :, None] * b_t[:, None, None, :]
        out_t = jnp.einsum('gshn,gn->gsh', stored, c_t, precision=lax.Precision.HIGHEST)
        return (stored, out_t)
    start_state = jnp.zeros((N_HEAD, SH, HP, NST), jnp.float32)
    ssm_y = lax.scan(advance, start_state, (decays, step_size, ssm_in, b_proj, c_proj))[1]
    ssm_y = ssm_y + skip_d.reshape(N_HEAD, SH)[None, :, :, None] * ssm_in
    gated = ssm_y.reshape(SEQUENCE_TOKENS, N_HEAD, ssm_width) * jax.nn.silu(gate_z)
    mean_sq = lax.optimization_barrier(jnp.mean(gated * gated, axis=-1, keepdims=True))
    normalized_input = (gated * lax.rsqrt(mean_sq + 1e-05) * ssm_gain.reshape(N_HEAD, ssm_width)).astype(jnp.bfloat16)
    features = jnp.concatenate([attn, normalized_input], axis=-1).reshape(SEQUENCE_TOKENS, N_HEAD * (q_width + ssm_width))
    mixed_seq = jnp.dot(features, w_out, preferred_element_type=jnp.float32).astype(jnp.bfloat16)
    return mixed_seq[positions]
```

```python
import functools
import math

import jax
import jax.numpy as jnp
from jax import lax
from jax.experimental import pallas as pl
from jax.experimental.pallas import tpu as pltpu
from jax.sharding import PartitionSpec as P

HD = 128
HP = 64
NST = 128
ROWS = 16
DOUT = 2560
N_YLO, N_Z, N_CORE, N_YHI, N_X = 4, 8, 2, 2, 4
MESH = pl.DeviceIdType.MESH
F32, BF16 = jnp.float32, jnp.bfloat16
NEG = -1e30
CUTS = 5


def nt_dot(a, b):
    return lax.dot_general(a, b, (((1,), (1,)), ((), ())), preferred_element_type=F32)


def nn_dot(a, b):
    return jnp.dot(a, b, preferred_element_type=F32)


def kernel(
    sizes,
    x_ref,
    skip_ref,
    gain_ref,
    w_hbm,
    out_ref,
    kv,
    qraw,
    q,
    feat,
    w_ref,
    vt,
    stat,
    acc,
    st_out,
    st_in,
    gt_out,
    gt,
    reach,
    carry_out,
    carry_in,
    o_out,
    os_out,
    o_in,
    os_in,
    comb,
    prod,
    rsx,
    red_out,
    keep,
    rsy,
    local_sem,
    a_send,
    a_recv,
    kv_send,
    kv_recv,
    fw_send,
    fw_recv,
    q_send,
    q_recv,
    st_send,
    st_recv,
    gt_send,
    gt_recv,
    ca_send,
    ca_recv,
    o_send,
    o_recv,
    x_send,
    x_recv,
    y_send,
    y_recv,
):
    ny, nz, nx = sizes
    nh, nj = 2 * nx, 2 * nz
    tok = nh * ROWS
    half = tok // 2
    group = 2 * half
    part = 128 // nj
    scale = math.log2(math.e) / math.sqrt(HD)
    order = [0]
    for d in range(1, nz // 2 + 1):
        order += [d] if 2 * d == nz else [d, nz - d]

    c, h = lax.axis_index("ctx"), lax.axis_index("head")
    a, j = c // nj, c % nj
    z, core = j // 2, j % 2
    yh, xx = h // nx, h % nx
    sends = []

    def push(src, dst, send_sem, recv_sem, device):
        copy = pltpu.make_async_remote_copy(
            src_ref=src,
            dst_ref=dst,
            send_sem=send_sem,
            recv_sem=recv_sem,
            device_id=device,
            device_id_type=MESH,
        )
        copy.start()
        sends.append(copy)

    def landed(dst, recv_sem):
        pltpu.make_async_copy(dst, dst, recv_sem).wait()

    def at_ylo(i):
        return (((a + i) % ny) * nj + j, h)

    def at_j(i):
        return (a * nj + (j + i) % nj, h)

    def at_z(d):
        return (a * nj + ((z + d) % nz) * 2 + core, h)

    def at_head(i):
        return (c, (h + i) % nh)

    def at_x(i):
        return (c, yh * nx + (xx + i) % nx)

    sibling = (a * nj + z * 2 + (1 - core), h)
    across = (c, (1 - yh) * nx + xx)

    w_copy = pltpu.make_async_copy(w_hbm, w_ref, local_sem.at[3])
    places = [
        (slice(256, 512), lambda s: kv.at[s // nx, 0, pl.ds(pl.multiple_of((s % nx) * ROWS, ROWS), ROWS), :]),
        (slice(0, 256), lambda s: qraw.at[pl.ds(pl.multiple_of(s * ROWS, ROWS), ROWS), :]),
        (slice(512, 1152), lambda s: feat.at[pl.ds(pl.multiple_of(s * ROWS, ROWS), ROWS), :]),
    ]
    own = []
    for n, (columns, place) in enumerate(places):
        copy = pltpu.make_async_copy(x_ref.at[h, :, columns], place(h), local_sem.at[n])
        copy.start()
        own.append(copy)
    w_copy.start()

    barrier = pltpu.get_barrier_semaphore()
    peers = [at_head(i) for i in range(1, nh)] + [at_j(i) for i in range(1, nj)] + [at_ylo(i) for i in range(1, ny)]
    for peer in peers:
        pl.semaphore_signal(barrier, inc=1, device_id=peer, device_id_type=MESH)
    pl.semaphore_wait(barrier, len(peers))

    for n, (columns, place) in enumerate(places):
        for i in range(1, nh):
            g = (h + i) % nh
            push(x_ref.at[g, :, columns], place(h), a_send.at[n, i], a_recv.at[n, i], at_head(i))

    def rows_in(n):
        own[n].wait()
        for i in range(1, nh):
            landed(places[n][1]((h + nh - i) % nh), a_recv.at[n, i])

    rows_in(0)
    push(kv.at[:, 0], kv.at[:, 1], fw_send.at[0], fw_recv.at[0], sibling)
    for e in range(1, nz):
        d = (nz - order[e]) % nz
        push(kv.at[:, 0], kv.at[:, 2 * e], kv_send.at[e], kv_recv.at[e], at_z(d))

    rows_in(1)
    for i in range(2):
        for n in range(2):
            q[0, i, n * half : (n + 1) * half, :] = qraw[i * half : (i + 1) * half, n * HD : (n + 1) * HD]
    for i in range(1, ny):
        push(q.at[0], q.at[ny - i], q_send.at[i], q_recv.at[i], at_ylo(i))

    rows_in(2)
    x_in = feat[:, 0:128]
    b_in = feat[:, 256:384]
    c_in = feat[:, 384:512]
    st = feat[:, 512:640]
    row_id = lax.broadcasted_iota(jnp.int32, (tok, tok), 0)
    col_id = lax.broadcasted_iota(jnp.int32, (tok, tok), 1)
    lower = (col_id <= row_id) & ((row_id < half) == (col_id < half))
    cum = nn_dot(jnp.where(lower, 1.0, 0.0).astype(BF16), st)
    st_f = st.astype(F32)
    lane = lax.broadcasted_iota(jnp.int32, (tok, 128), 1)
    early_row = lax.broadcasted_iota(jnp.int32, (tok, 128), 0) < half
    first_head = lane < HP
    total_e, total_l = cum[half - 1 : half, :], cum[tok - 1 : tok, :]
    to_end = jnp.exp(jnp.where(early_row, total_e, total_l) - cum)
    weigh = jnp.where(first_head, to_end[:, 2:3] * st_f[:, 0:1], to_end[:, 3:4] * st_f[:, 1:2])
    x_f = x_in.astype(F32)
    xs_t = (x_f * weigh).T
    early_lane = lax.broadcasted_iota(jnp.int32, (128, tok), 1) < half
    piece_e = nn_dot(jnp.where(early_lane, xs_t, 0.0).astype(BF16), b_in)
    piece_l = nn_dot(jnp.where(early_lane, 0.0, xs_t).astype(BF16), b_in)
    st_out[:, 0:part, :] = piece_e.reshape(nj, part, NST)
    st_out[:, part : 2 * part, :] = piece_l.reshape(nj, part, NST)
    upper_rows = lax.broadcasted_iota(jnp.int32, (8, 128), 0) < 4
    for s in range(2):
        tile = jnp.exp(
            jnp.where(
                upper_rows,
                jnp.broadcast_to(total_e[:, 2 + s : 3 + s], (8, 128)),
                jnp.broadcast_to(total_l[:, 2 + s : 3 + s], (8, 128)),
            )
        )
        st_out[s * (nj // 2) : (s + 1) * (nj // 2), 2 * part :, :] = jnp.broadcast_to(tile[None], (nj // 2, 8, 128))
    for i in range(1, nj):
        push(st_out.at[(j + i) % nj], st_in.at[j], st_send.at[i], st_recv.at[i], at_j(i))
    st_in[j] = st_out[j]

    cum_t, st_t = cum.T, st_f.T
    pairs = nt_dot(c_in, b_in)
    within = []
    for s in range(2):
        gap = jnp.where(lower, cum[:, 2 + s : 3 + s] - cum_t[2 + s : 3 + s, :], NEG)
        mix = jnp.exp(gap) * pairs * st_t[s : s + 1, :]
        within.append(nn_dot(mix.astype(BF16), x_in))
    skip = jnp.where(first_head, skip_ref[0], skip_ref[1])
    intra = jnp.where(first_head, within[0], within[1]) + skip * x_f

    def forward(e):
        landed(kv.at[:, 2 * e], kv_recv.at[e])
        push(kv.at[:, 2 * e], kv.at[:, 2 * e + 1], fw_send.at[e], fw_recv.at[e], sibling)

    key_row = lax.broadcasted_iota(jnp.int32, (4 * half, group), 0)
    q_tok = lax.broadcasted_iota(jnp.int32, (4 * half, group), 1) % half
    picked = [None] + [jnp.where(a + i < ny, 0, 1) for i in range(1, ny)]

    def absorb(scores, values_t, lanes, first):
        top = jnp.max(scores, axis=0, keepdims=True)
        if not first:
            before = stat[0:1, lanes]
            top = jnp.maximum(top, before)
        probs = jnp.exp2(scores * scale - top * scale)
        total = jnp.sum(probs, axis=0, keepdims=True)
        added = nn_dot(values_t, probs.astype(BF16))
        if not first:
            shrink = jnp.exp2((before - top) * scale)
            total = total + stat[1:2, lanes] * shrink
            added = added + acc[:, lanes] * shrink
        stat[0:1, lanes] = top
        stat[1:2, lanes] = total
        acc[:, lanes] = added

    def attend(n):
        first = n == 0
        slots = slice(4 * n, 4 * n + 4)
        for i in range(2):
            vt[i] = kv[i, slots, :, HD : 2 * HD].reshape(4 * half, HD).T
        keys_e = kv[0, slots, :, 0:HD].reshape(4 * half, HD)
        keys_l = kv[1, slots, :, 0:HD].reshape(4 * half, HD)
        absorb(nt_dot(keys_e, q[:, 1].reshape(ny * group, HD)), vt[0], slice(0, ny * group), first)
        for i in range(1, ny):
            s = picked[i]
            at = (ny + i - 1) * group
            keys = kv[s, slots, :, 0:HD].reshape(4 * half, HD)
            absorb(nt_dot(keys, q[i, s]), vt[s], slice(at, at + group), first)
        block = jnp.zeros((4 * half, group), jnp.int32)
        for m in range(4):
            from_z = (z + order[2 * n + m // 2]) % nz
            from_core = core if m % 2 == 0 else 1 - core
            block = jnp.where(key_row // half == m, from_z * 2 + from_core, block)
        key_tok = key_row % half
        see_e = block * half + key_tok <= j * half + q_tok
        see_l = (nj - 1 - block) * half + key_tok <= (nj - 1 - j) * half + q_tok
        at = (2 * ny - 1) * group
        absorb(jnp.where(see_e, nt_dot(keys_e, q[0, 0]), NEG), vt[0], slice(at, at + group), first)
        at = 2 * ny * group
        absorb(jnp.where(see_l, nt_dot(keys_l, q[0, 1]), NEG), vt[1], slice(at, at + group), first)

    def chunk(n):
        for e in (2 * n, 2 * n + 1):
            landed(kv.at[:, 2 * e + 1], fw_recv.at[e])
        attend(n)

    def states_in():
        for i in range(1, nj):
            landed(st_in.at[(j + nj - i) % nj], st_recv.at[i])
        state = jnp.zeros((part, NST), F32)
        decay = jnp.ones((1, NST), F32)
        for k in range(nj):
            carry_out[k, 0:part, :] = state
            reach[k, 0:1, :] = decay
            d = st_in[k, 2 * part : 2 * part + 1, :]
            state = d * state + st_in[k, 0:part, :]
            decay = d * decay
        gt_out[0:part, :] = state
        gt_out[2 * part : 2 * part + 4, :] = jnp.broadcast_to(decay, (4, NST))
        state = jnp.zeros((part, NST), F32)
        decay = jnp.ones((1, NST), F32)
        for k in reversed(range(nj)):
            carry_out[k, part : 2 * part, :] = state
            reach[k, 1:2, :] = decay
            d = st_in[k, 2 * part + 4 : 2 * part + 5, :]
            state = d * state + st_in[k, part : 2 * part, :]
            decay = d * decay
        gt_out[part : 2 * part, :] = state
        gt_out[2 * part + 4 : 2 * part + 8, :] = jnp.broadcast_to(decay, (4, NST))
        for i in range(1, ny):
            push(gt_out, gt.at[a], gt_send.at[i], gt_recv.at[i], at_ylo(i))
        gt[a] = gt_out[...]

    def carries_out():
        for i in range(1, ny):
            landed(gt.at[(a + ny - i) % ny], gt_recv.at[i])
        enter_e = jnp.zeros((part, NST), F32)
        enter_l = jnp.zeros((part, NST), F32)
        state = jnp.zeros((part, NST), F32)
        for g in range(ny):
            enter_e = jnp.where(a == g, state, enter_e)
            state = gt[g, 2 * part : 2 * part + 1, :] * state + gt[g, 0:part, :]
        for g in reversed(range(ny)):
            enter_l = jnp.where(a == g, state, enter_l)
            state = gt[g, 2 * part + 4 : 2 * part + 5, :] * state + gt[g, part : 2 * part, :]
        for k in range(nj):
            carry_out[k, 0:part, :] += reach[k, 0:1, :] * enter_e
            carry_out[k, part : 2 * part, :] += reach[k, 1:2, :] * enter_l
        for i in range(1, nj):
            push(carry_out.at[(j + i) % nj], carry_in.at[j], ca_send.at[i], ca_recv.at[i], at_j(i))
        carry_in[j] = carry_out[j]

    chunks = nz // 2
    forward(1)
    for i in range(1, ny):
        landed(q.at[ny - i], q_recv.at[i])
    if nz > 2:
        forward(2)
    chunk(0)
    states_in()
    for n in range(1, chunks):
        forward(2 * n + 1)
        if n + 1 < chunks:
            forward(2 * n + 2)
        if n == 1:
            carries_out()
        chunk(n)
    if chunks == 1:
        carries_out()

    for i in range(1, ny):
        for n, at in enumerate((i * group, (ny + i - 1) * group)):
            o_out[i - 1, n] = acc[:, at : at + group].astype(BF16)
            os_out[i - 1, 2 * n : 2 * n + 2, :] = stat[0:2, at : at + group]
        os_out[i - 1, 4:8, :] = jnp.zeros((4, group), F32)
        push(os_out.at[i - 1], os_in.at[ny - i - 1], o_send.at[0, i], o_recv.at[0, i], at_ylo(i))
        push(o_out.at[i - 1], o_in.at[ny - i - 1], o_send.at[1, i], o_recv.at[1, i], at_ylo(i))

    for i in range(1, nj):
        landed(carry_in.at[(j + nj - i) % nj], ca_recv.at[i])
    carry_e = carry_in[:, 0:part, :].reshape(128, NST).astype(BF16)
    carry_l = carry_in[:, part : 2 * part, :].reshape(128, NST).astype(BF16)
    inter = jnp.where(early_row, nt_dot(c_in, carry_e), nt_dot(c_in, carry_l))
    ssm_y = intra + inter * jnp.exp(jnp.where(first_head, cum[:, 2:3], cum[:, 3:4]))
    gate = feat[:, 128:256].astype(F32)
    gated = ssm_y * (gate / (1.0 + jnp.exp(-gate)))
    mean_sq = jnp.mean(gated * gated, axis=1, keepdims=True)
    comb[:, 2 * HD : 3 * HD] = (gated * lax.rsqrt(mean_sq + 1e-05) * gain_ref[...]).astype(BF16)

    def unit(n):
        lanes = slice(n * group, (n + 1) * group)
        return stat[0:1, lanes], stat[1:2, lanes], acc[:, lanes]

    early, late = [unit(2 * ny - 1)], [unit(0), unit(2 * ny)]
    for i in range(1, ny):
        landed(os_in.at[ny - i - 1], o_recv.at[0, i])
        landed(o_in.at[ny - i - 1], o_recv.at[1, i])
    for i in range(1, ny):
        s = os_in[i - 1]
        late.append((s[0:1], s[1:2], o_in[i - 1, 0].astype(F32)))
        is_early = a + i >= ny
        other = o_in[i - 1, 1].astype(F32)
        early.append((jnp.where(is_early, s[2:3], NEG), s[3:4], other))
        late.append((jnp.where(is_early, NEG, s[2:3]), s[3:4], other))
    for n, parts in enumerate((early, late)):
        top = functools.reduce(jnp.maximum, [p[0] for p in parts])
        total, weighted = 0.0, 0.0
        for m, l, o in parts:
            w = jnp.exp2((m - top) * scale)
            total = total + w * l
            weighted = weighted + w * o
        attn = (weighted / total).T.astype(BF16)
        rows = slice(n * half, (n + 1) * half)
        comb[rows, 0:HD] = attn[0:half]
        comb[rows, HD : 2 * HD] = attn[half:]

    w_copy.wait()
    width = DOUT // CUTS
    for n in range(CUTS):
        share = nn_dot(comb[...], w_ref[:, n * width : (n + 1) * width]).astype(BF16)
        prod[n] = share.reshape(2, nx, ROWS, width)
        for i in range(1, nx):
            push(
                prod.at[n, :, (xx + i) % nx],
                rsx.at[n, nx - i - 1],
                x_send.at[n, i],
                x_recv.at[n, i],
                at_x(i),
            )
    for n in range(CUTS):
        for i in range(1, nx):
            landed(rsx.at[n, nx - i - 1], x_recv.at[n, i])
        mine = prod[n, yh, xx].astype(F32)
        other = prod[n, 1 - yh, xx].astype(F32)
        for i in range(nx - 1):
            mine = mine + rsx[n, i, yh].astype(F32)
            other = other + rsx[n, i, 1 - yh].astype(F32)
        red_out[n] = other.astype(BF16)
        push(red_out.at[n], rsy.at[n], y_send.at[n], y_recv.at[n], across)
        keep[n] = mine
    for n in range(CUTS):
        landed(rsy.at[n], y_recv.at[n])
        out_ref[:, n * width : (n + 1) * width] = (keep[n] + rsy[n].astype(F32)).astype(BF16)
    for copy in sends:
        copy.wait_send()


def make(sizes):
    ny, nz, nx = sizes
    nh, nj = 2 * nx, 2 * nz
    tok = nh * ROWS
    half = tok // 2
    group = 2 * half
    part = 128 // nj
    width = DOUT // CUTS
    units = 2 * ny + 1

    def body(streams, steps, skip_d, ssm_gain, w_out):
        padded = jnp.pad(steps, ((0, 0), (0, 0), (0, 128 - steps.shape[2])))
        x = jnp.concatenate([streams, padded], axis=2).transpose(1, 0, 2)
        dma = pltpu.SemaphoreType.DMA
        scratch = dict(
            kv=pltpu.VMEM((2, 2 * nz, half, 2 * HD), BF16),
            qraw=pltpu.VMEM((tok, 2 * HD), BF16),
            q=pltpu.VMEM((ny, 2, group, HD), BF16),
            feat=pltpu.VMEM((tok, 640), BF16),
            w_ref=pltpu.VMEM((3 * HD, DOUT), BF16),
            vt=pltpu.VMEM((2, HD, 4 * half), BF16),
            stat=pltpu.VMEM((8, units * group), F32),
            acc=pltpu.VMEM((HD, units * group), F32),
            st_out=pltpu.VMEM((nj, 2 * part + 8, NST), F32),
            st_in=pltpu.VMEM((nj, 2 * part + 8, NST), F32),
            gt_out=pltpu.VMEM((2 * part + 8, NST), F32),
            gt=pltpu.VMEM((ny, 2 * part + 8, NST), F32),
            reach=pltpu.VMEM((nj, 8, NST), F32),
            carry_out=pltpu.VMEM((nj, 2 * part, NST), F32),
            carry_in=pltpu.VMEM((nj, 2 * part, NST), F32),
            o_out=pltpu.VMEM((ny - 1, 2, HD, group), BF16),
            os_out=pltpu.VMEM((ny - 1, 8, group), F32),
            o_in=pltpu.VMEM((ny - 1, 2, HD, group), BF16),
            os_in=pltpu.VMEM((ny - 1, 8, group), F32),
            comb=pltpu.VMEM((tok, 3 * HD), BF16),
            prod=pltpu.VMEM((CUTS, 2, nx, ROWS, width), BF16),
            rsx=pltpu.VMEM((CUTS, nx - 1, 2, ROWS, width), BF16),
            red_out=pltpu.VMEM((CUTS, ROWS, width), BF16),
            keep=pltpu.VMEM((CUTS, ROWS, width), F32),
            rsy=pltpu.VMEM((CUTS, ROWS, width), BF16),
            local_sem=dma((4,)),
            a_send=dma((3, nh)),
            a_recv=dma((3, nh)),
            kv_send=dma((nz,)),
            kv_recv=dma((nz,)),
            fw_send=dma((nz,)),
            fw_recv=dma((nz,)),
            q_send=dma((ny,)),
            q_recv=dma((ny,)),
            st_send=dma((nj,)),
            st_recv=dma((nj,)),
            gt_send=dma((ny,)),
            gt_recv=dma((ny,)),
            ca_send=dma((nj,)),
            ca_recv=dma((nj,)),
            o_send=dma((2, ny)),
            o_recv=dma((2, ny)),
            x_send=dma((CUTS, nx)),
            x_recv=dma((CUTS, nx)),
            y_send=dma((CUTS,)),
            y_recv=dma((CUTS,)),
        )
        return pl.pallas_call(
            functools.partial(kernel, sizes),
            out_shape=jax.ShapeDtypeStruct((ROWS, DOUT), BF16),
            in_specs=[
                pl.BlockSpec(memory_space=pl.ANY),
                pl.BlockSpec(memory_space=pltpu.SMEM),
                pl.BlockSpec(memory_space=pltpu.VMEM),
                pl.BlockSpec(memory_space=pl.ANY),
            ],
            out_specs=pl.BlockSpec(memory_space=pltpu.VMEM),
            scratch_shapes=list(scratch.values()),
            compiler_params=pltpu.CompilerParams(
                collective_id=0, has_side_effects=True, vmem_limit_bytes=48 * 1024 * 1024
            ),
        )(x, skip_d, ssm_gain.reshape(1, 128), w_out)

    return body


def solution(mesh):
    return jax.shard_map(
        make((N_YLO, N_Z, N_X)),
        mesh=mesh,
        in_specs=(
            P(("ctx", "head"), None, None),
            P(("ctx", "head"), None, None),
            P("head"),
            P("head"),
            P("head", None),
        ),
        out_specs=P(("ctx", "head"), None),
        check_vma=False,
    )
```

```python
import functools
import math

import jax
import jax.numpy as jnp
from jax import lax
from jax.experimental import pallas as pl
from jax.experimental.pallas import tpu as pltpu
from jax.sharding import PartitionSpec as P

HD = 128
HP = 64
NST = 128
ROWS = 16
DOUT = 2560
N_YLO, N_Z, N_CORE, N_YHI, N_X = 4, 8, 2, 2, 4
MESH = pl.DeviceIdType.MESH
F32, BF16 = jnp.float32, jnp.bfloat16
NEG = -1e30
CUTS = 2
LEAVE = (0, 1, 2, 3)
PLAN = (
    "keys0",
    "keys1",
    "queries",
    "pieces",
    "slices",
    "pass01",
    "pass02",
    "pass03",
    "pass04",
    "pass05",
    "pass06",
    "pass07",
    "intra",
    "pass11",
    "attend0",
    "pass12",
    "pass13",
    "attend1",
    "states",
    "pass14",
    "pass15",
    "attend2",
    "carries",
    "pass16",
    "pass17",
    "attend3",
)


def nt_dot(a, b):
    return lax.dot_general(a, b, (((1,), (1,)), ((), ())), preferred_element_type=F32)


def nn_dot(a, b):
    return jnp.dot(a, b, preferred_element_type=F32)


def kernel(
    sizes,
    x_ref,
    steps_hbm,
    skip_hbm,
    gain_hbm,
    w_hbm,
    out_ref,
    kv,
    qraw,
    q,
    feat,
    steps_ref,
    steps_out,
    steps_in,
    skip_ref,
    gain_ref,
    w_ref,
    vt,
    stat,
    acc,
    pair_out,
    pair_in,
    st_out,
    st_in,
    gt_out,
    gt,
    enter,
    reach,
    carry_out,
    carry_in,
    next_out,
    next_in,
    o_out,
    os_out,
    o_in,
    os_in,
    comb,
    prod,
    rsx,
    red_out,
    rsy,
    local_sem,
    a_send,
    a_recv,
    kv_send,
    kv_recv,
    fw_send,
    fw_recv,
    q_send,
    q_recv,
    pair_send,
    pair_recv,
    st_send,
    st_recv,
    gt_send,
    gt_recv,
    ca_send,
    ca_recv,
    o_send,
    o_recv,
    x_send,
    x_recv,
    y_send,
    y_recv,
):
    ny, nz, nx = sizes
    nh, nj = 2 * nx, 2 * nz
    tok = nh * ROWS
    half = tok // 2
    group = 2 * half
    part = 128 // nz
    scale = math.log2(math.e) / math.sqrt(HD)
    order = [0]
    for d in range(1, nz // 2 + 1):
        order += [d] if 2 * d == nz else [d, nz - d]

    c, h = lax.axis_index("ctx"), lax.axis_index("head")
    a, j = c // nj, c % nj
    z, core = j // 2, j % 2
    yh, xx = h // nx, h % nx
    sends = []

    def push(src, dst, send_sem, recv_sem, device):
        copy = pltpu.make_async_remote_copy(
            src_ref=src,
            dst_ref=dst,
            send_sem=send_sem,
            recv_sem=recv_sem,
            device_id=device,
            device_id_type=MESH,
        )
        copy.start()
        sends.append(copy)

    def landed(dst, recv_sem):
        pltpu.make_async_copy(dst, dst, recv_sem).wait()

    def at_ylo(i):
        return (((a + i) % ny) * nj + j, h)

    def at_ylo_other(i):
        return (((a + i) % ny) * nj + z * 2 + (1 - core), h)

    def at_z(d):
        return (a * nj + ((z + d) % nz) * 2 + core, h)

    def at_head(i):
        return (c, (h + i) % nh)

    def at_x(i):
        return (c, yh * nx + (xx + i) % nx)

    sibling = (a * nj + z * 2 + (1 - core), h)
    across = (c, (1 - yh) * nx + xx)

    steps_copy = pltpu.make_async_copy(steps_hbm, steps_ref, local_sem.at[3])
    steps_copy.start()
    places = [
        (slice(256, 512), lambda s: kv.at[s // nx, 0, pl.ds(pl.multiple_of((s % nx) * ROWS, ROWS), ROWS), :]),
        (slice(0, 256), lambda s: qraw.at[pl.ds(pl.multiple_of(s * ROWS, ROWS), ROWS), :]),
        (slice(512, 1024), lambda s: feat.at[pl.ds(pl.multiple_of(s * ROWS, ROWS), ROWS), :]),
    ]
    own = []
    for n, (columns, place) in enumerate(places):
        copy = pltpu.make_async_copy(x_ref.at[h, :, columns], place(h), local_sem.at[n])
        copy.start()
        own.append(copy)
    skip_copy = pltpu.make_async_copy(skip_hbm, skip_ref, local_sem.at[4])
    skip_copy.start()
    gain_copy = pltpu.make_async_copy(gain_hbm, gain_ref, local_sem.at[5])
    gain_copy.start()
    w_copy = pltpu.make_async_copy(w_hbm, w_ref, local_sem.at[6])
    w_copy.start()

    barrier = pltpu.get_barrier_semaphore()
    peers = [at_head(i) for i in range(1, nh)] + [at_z(d) for d in range(1, nz)] + [sibling]
    peers += [at_ylo(i) for i in range(1, ny)] + [at_ylo_other(i) for i in range(1, ny)]
    for peer in peers:
        pl.semaphore_signal(barrier, inc=1, device_id=peer, device_id_type=MESH)
    pl.semaphore_wait(barrier, len(peers))

    def features_out(n):
        columns, place = places[n]
        for i in range(1, nh):
            g = (h + i) % nh
            push(x_ref.at[g, :, columns], place(h), a_send.at[n, i], a_recv.at[n, i], at_head(i))

    def steps_go():
        steps_copy.wait()
        steps_out[...] = jnp.zeros((nh, 8, 128), F32)
        steps_out[:, 0:4, 0:ROWS] = steps_ref[...].astype(F32)
        for i in range(1, nh):
            push(steps_out.at[(h + i) % nh], steps_in.at[h], a_send.at[3, i], a_recv.at[3, i], at_head(i))
        steps_in[h] = steps_out[h]

    for n in LEAVE:
        if n == 3:
            steps_go()
        else:
            features_out(n)

    def rows_in(n):
        own[n].wait()
        for i in range(1, nh):
            landed(places[n][1]((h + nh - i) % nh), a_recv.at[n, i])

    halves = (yh, 1 - yh)

    def keys(n):
        if n == 0:
            own[0].wait()
        for i in range(n == 0, nx):
            s = halves[n] * nx + (xx + i) % nx
            landed(places[0][1](s), a_recv.at[0, (h + nh - s) % nh])
        mine = kv.at[halves[n], 0]
        for e in range(1, nz):
            push(mine, kv.at[halves[n], 2 * e], kv_send.at[n, e], kv_recv.at[n, e], at_z(nz - order[e]))
        push(mine, kv.at[halves[n], 1], fw_send.at[n, 0], fw_recv.at[n, 0], sibling)

    def pass_on(n, e):
        block = kv.at[halves[n], 2 * e]
        landed(block, kv_recv.at[n, e])
        push(block, kv.at[halves[n], 2 * e + 1], fw_send.at[n, e], fw_recv.at[n, e], sibling)

    def queries():
        rows_in(1)
        for i in range(2):
            for n in range(2):
                q[0, i, n * half : (n + 1) * half, :] = qraw[i * half : (i + 1) * half, n * HD : (n + 1) * HD]
        for i in range(1, ny):
            push(q.at[0], q.at[ny - i], q_send.at[i], q_recv.at[i], at_ylo(i))

    row_id = lax.broadcasted_iota(jnp.int32, (tok, tok), 0)
    col_id = lax.broadcasted_iota(jnp.int32, (tok, tok), 1)
    lower = (col_id <= row_id) & ((row_id < half) == (col_id < half))
    early_row = lax.broadcasted_iota(jnp.int32, (tok, 128), 0) < half
    first_head = lax.broadcasted_iota(jnp.int32, (tok, 128), 1) < HP
    is_early_core = core == 0
    known = {}

    def pieces():
        rows_in(2)
        for i in range(1, nh):
            landed(steps_in.at[(h + nh - i) % nh], a_recv.at[3, i])
        st_t = steps_in[0]
        for g in range(1, nh):
            st_t = st_t + pltpu.roll(steps_in[g], g * ROWS, 1)
        st_t = st_t[:, 0:tok]
        st_f = jnp.concatenate([st_t, jnp.zeros((120, tok), F32)], axis=0).T
        cum = nn_dot(jnp.where(lower, 1.0, 0.0).astype(BF16), st_f.astype(BF16))
        total_e, total_l = cum[half - 1 : half, :], cum[tok - 1 : tok, :]
        to_end = jnp.exp(jnp.where(early_row, total_e, total_l) - cum)
        weigh = jnp.where(first_head, to_end[:, 2:3] * st_f[:, 0:1], to_end[:, 3:4] * st_f[:, 1:2])
        x_in, b_in = feat[:, 0:128], feat[:, 256:384]
        xs_t = (x_in.astype(F32) * weigh).T
        early_lane = lax.broadcasted_iota(jnp.int32, (128, tok), 1) < half
        piece_e = nn_dot(jnp.where(early_lane, xs_t, 0.0).astype(BF16), b_in)
        piece_l = nn_dot(jnp.where(early_lane, 0.0, xs_t).astype(BF16), b_in)
        head_rows = lax.broadcasted_iota(jnp.int32, (128, 128), 0) < HP
        decay_e, decay_l = (
            jnp.exp(jnp.where(head_rows, t[:, 2:3], t[:, 3:4])) for t in (total_e, total_l)
        )
        pair_out[0] = jnp.where(is_early_core, piece_l, piece_e)
        pair_out[1] = jnp.where(is_early_core, decay_l, decay_e)
        push(pair_out, pair_in, pair_send.at[0], pair_recv.at[0], sibling)
        known["piece"] = jnp.where(is_early_core, piece_e, piece_l)
        known["decay"] = jnp.where(is_early_core, decay_e, decay_l)
        known["cum"], known["st_t"] = cum, st_t

    def slices():
        landed(pair_in, pair_recv.at[0])
        both = pair_in[1] * known["piece"] + pair_in[0]
        decay = pair_in[1] * known["decay"]
        st_out[:, 0:part, :] = both.reshape(nz, part, NST)
        st_out[:, part:, :] = decay.reshape(nz, part, NST)[:, 0:8, :]
        for d in range(1, nz):
            push(st_out.at[(z + d) % nz], st_in.at[z], st_send.at[d], st_recv.at[d], at_z(d))
        st_in[z] = st_out[z]

    def intra():
        x_in, b_in, c_in = feat[:, 0:128], feat[:, 256:384], feat[:, 384:512]
        cum, st_t = known["cum"], known["st_t"]
        cum_t = cum.T
        pairs = nt_dot(c_in, b_in)
        within = []
        for s in range(2):
            gap = jnp.where(lower, cum[:, 2 + s : 3 + s] - cum_t[2 + s : 3 + s, :], NEG)
            mix = jnp.exp(gap) * pairs * st_t[s : s + 1, :]
            within.append(nn_dot(mix.astype(BF16), x_in))
        skip_copy.wait()
        skip = jnp.where(first_head, skip_ref[0:1, 0:1], skip_ref[0:1, 1:2])
        known["intra"] = jnp.where(first_head, within[0], within[1]) + skip * x_in.astype(F32)

    key_row = lax.broadcasted_iota(jnp.int32, (4 * half, group), 0)
    q_tok = lax.broadcasted_iota(jnp.int32, (4 * half, group), 1) % half
    picked = [None] + [jnp.where(a + i < ny, 0, 1) for i in range(1, ny)]

    def absorb(scores, values_t, lanes, first):
        top = jnp.max(scores, axis=0, keepdims=True)
        if not first:
            before = stat[0:1, lanes]
            top = jnp.maximum(top, before)
        probs = jnp.exp2(scores * scale - top * scale)
        total = jnp.sum(probs, axis=0, keepdims=True)
        added = nn_dot(values_t, probs.astype(BF16))
        if not first:
            shrink = jnp.exp2((before - top) * scale)
            total = total + stat[1:2, lanes] * shrink
            added = added + acc[:, lanes] * shrink
        stat[0:1, lanes] = top
        stat[1:2, lanes] = total
        acc[:, lanes] = added

    def attend(n):
        first = n == 0
        slots = slice(4 * n, 4 * n + 4)
        for i in range(2):
            vt[i] = kv[i, slots, :, HD : 2 * HD].reshape(4 * half, HD).T
        keys_e = kv[0, slots, :, 0:HD].reshape(4 * half, HD)
        keys_l = kv[1, slots, :, 0:HD].reshape(4 * half, HD)
        absorb(nt_dot(keys_e, q[:, 1].reshape(ny * group, HD)), vt[0], slice(0, ny * group), first)
        for i in range(1, ny):
            s = picked[i]
            at = (ny + i - 1) * group
            keys = kv[s, slots, :, 0:HD].reshape(4 * half, HD)
            absorb(nt_dot(keys, q[i, s]), vt[s], slice(at, at + group), first)
        block = jnp.zeros((4 * half, group), jnp.int32)
        for m in range(4):
            from_z = (z + order[2 * n + m // 2]) % nz
            from_core = core if m % 2 == 0 else 1 - core
            block = jnp.where(key_row // half == m, from_z * 2 + from_core, block)
        key_tok = key_row % half
        see_e = block * half + key_tok <= j * half + q_tok
        see_l = (nj - 1 - block) * half + key_tok <= (nj - 1 - j) * half + q_tok
        at = (2 * ny - 1) * group
        absorb(jnp.where(see_e, nt_dot(keys_e, q[0, 0]), NEG), vt[0], slice(at, at + group), first)
        at = 2 * ny * group
        absorb(jnp.where(see_l, nt_dot(keys_l, q[0, 1]), NEG), vt[1], slice(at, at + group), first)

    def chunk(n):
        if n == 0:
            for i in range(1, ny):
                landed(q.at[ny - i], q_recv.at[i])
        for e in (2 * n, 2 * n + 1):
            for i in range(2):
                landed(kv.at[halves[i], 2 * e + 1], fw_recv.at[i, e])
        attend(n)

    def states_in():
        for d in range(1, nz):
            landed(st_in.at[(z + nz - d) % nz], st_recv.at[d])
        state = jnp.zeros((part, NST), F32)
        decay = jnp.ones((1, NST), F32)
        for k in range(nz):
            at = jnp.where(is_early_core, k, nz - 1 - k)
            enter[at] = state
            reach[at] = jnp.broadcast_to(decay, (8, NST))
            arrived = st_in[at]
            state = arrived[part : part + 1] * state + arrived[0:part]
            decay = arrived[part : part + 1] * decay
        gt_out[0:part, :] = state
        gt_out[part:, :] = jnp.broadcast_to(decay, (8, NST))
        for i in range(1, ny):
            push(gt_out, gt.at[core, a], gt_send.at[0, i], gt_recv.at[0, i], at_ylo(i))
            push(gt_out, gt.at[core, a], gt_send.at[1, i], gt_recv.at[1, i], at_ylo_other(i))
        push(gt_out, gt.at[core, a], gt_send.at[1, 0], gt_recv.at[1, 0], sibling)
        gt[core, a] = gt_out[...]

    def carries_out():
        for i in range(1, ny):
            landed(gt.at[core, (a + ny - i) % ny], gt_recv.at[0, i])
            landed(gt.at[1 - core, (a + ny - i) % ny], gt_recv.at[1, i])
        landed(gt.at[1 - core, a], gt_recv.at[1, 0])
        first = jnp.zeros((part, NST), F32)
        state = jnp.zeros((part, NST), F32)
        for g in range(ny):
            first = jnp.where(is_early_core & (a == g), state, first)
            state = gt[0, g, part : part + 1, :] * state + gt[0, g, 0:part, :]
        for g in reversed(range(ny)):
            first = jnp.where(jnp.logical_not(is_early_core) & (a == g), state, first)
            state = gt[1, g, part : part + 1, :] * state + gt[1, g, 0:part, :]
        for k in range(nz):
            carry_out[k] = (enter[k] + reach[k, 0:1, :] * first).astype(BF16)
        for d in range(1, nz):
            push(carry_out.at[(z + d) % nz], carry_in.at[z], ca_send.at[d], ca_recv.at[d], at_z(d))
        carry_in[z] = carry_out[z]

    def next_state():
        for d in range(1, nz):
            landed(carry_in.at[(z + nz - d) % nz], ca_recv.at[d])
        into = carry_in[...].reshape(128, NST)
        next_out[...] = (known["decay"] * into.astype(F32) + known["piece"]).astype(BF16)
        push(next_out, next_in, pair_send.at[1], pair_recv.at[1], sibling)
        return into

    steps = {"queries": queries, "pieces": pieces, "slices": slices, "intra": intra}
    steps |= {"states": states_in, "carries": carries_out}
    steps |= {f"keys{n}": functools.partial(keys, n) for n in range(2)}
    steps |= {f"pass{n}{e}": functools.partial(pass_on, n, e) for n in range(2) for e in range(1, nz)}
    steps |= {f"attend{n}": functools.partial(chunk, n) for n in range(nz // 2)}
    for name in PLAN:
        if name in steps:
            steps[name]()

    for i in range(1, ny):
        for n, at in enumerate((i * group, (ny + i - 1) * group)):
            o_out[i - 1, n] = acc[:, at : at + group].astype(BF16)
            os_out[i - 1, 2 * n : 2 * n + 2, :] = stat[0:2, at : at + group]
        os_out[i - 1, 4:8, :] = jnp.zeros((4, group), F32)
        push(os_out.at[i - 1], os_in.at[ny - i - 1], o_send.at[0, i], o_recv.at[0, i], at_ylo(i))
        push(o_out.at[i - 1], o_in.at[ny - i - 1], o_send.at[1, i], o_recv.at[1, i], at_ylo(i))

    into = next_state()
    landed(next_in, pair_recv.at[1])
    carry_e = jnp.where(is_early_core, into, next_in[...])
    carry_l = jnp.where(is_early_core, next_in[...], into)
    c_in = feat[:, 384:512]
    inter = jnp.where(early_row, nt_dot(c_in, carry_e), nt_dot(c_in, carry_l))
    cum = known["cum"]
    ssm_y = known["intra"] + inter * jnp.exp(jnp.where(first_head, cum[:, 2:3], cum[:, 3:4]))
    gate = feat[:, 128:256].astype(F32)
    gated = ssm_y * (gate / (1.0 + jnp.exp(-gate)))
    mean_sq = jnp.mean(gated * gated, axis=1, keepdims=True)
    gain_copy.wait()
    comb[:, 2 * HD : 3 * HD] = (gated * lax.rsqrt(mean_sq + 1e-05) * gain_ref[...]).astype(BF16)

    def unit(n):
        lanes = slice(n * group, (n + 1) * group)
        return stat[0:1, lanes], stat[1:2, lanes], acc[:, lanes]

    early, late = [unit(2 * ny - 1)], [unit(0), unit(2 * ny)]
    for i in range(1, ny):
        landed(os_in.at[ny - i - 1], o_recv.at[0, i])
        landed(o_in.at[ny - i - 1], o_recv.at[1, i])
    for i in range(1, ny):
        s = os_in[i - 1]
        late.append((s[0:1], s[1:2], o_in[i - 1, 0].astype(F32)))
        is_early = a + i >= ny
        other = o_in[i - 1, 1].astype(F32)
        early.append((jnp.where(is_early, s[2:3], NEG), s[3:4], other))
        late.append((jnp.where(is_early, NEG, s[2:3]), s[3:4], other))
    for n, parts in enumerate((early, late)):
        top = functools.reduce(jnp.maximum, [p[0] for p in parts])
        total, weighted = 0.0, 0.0
        for m, l, o in parts:
            w = jnp.exp2((m - top) * scale)
            total = total + w * l
            weighted = weighted + w * o
        attn = (weighted / total).T.astype(BF16)
        rows = slice(n * half, (n + 1) * half)
        comb[rows, 0:HD] = attn[0:half]
        comb[rows, HD : 2 * HD] = attn[half:]

    w_copy.wait()
    width = DOUT // CUTS

    def over_x(n, way):
        for i in range(1, nx):
            push(
                prod.at[n, halves[1 - way], (xx + i) % nx],
                rsx.at[n, nx - i - 1, way],
                x_send.at[n, way, i],
                x_recv.at[n, way, i],
                at_x(i),
            )

    def sum_over_x(n, way):
        for i in range(1, nx):
            landed(rsx.at[n, nx - i - 1, way], x_recv.at[n, way, i])
        total = prod[n, halves[1 - way], xx].astype(F32)
        for i in range(nx - 1):
            total = total + rsx[n, i, way].astype(F32)
        return total

    for n in range(CUTS):
        share = nn_dot(comb[...], w_ref[:, n * width : (n + 1) * width]).astype(BF16)
        prod[n] = share.reshape(2, nx, ROWS, width)
        over_x(n, 0)
    for n in range(CUTS):
        red_out[n] = sum_over_x(n, 0).astype(BF16)
        push(red_out.at[n], rsy.at[n], y_send.at[n], y_recv.at[n], across)
        over_x(n, 1)
    for n in range(CUTS):
        total = sum_over_x(n, 1)
        landed(rsy.at[n], y_recv.at[n])
        out_ref[:, n * width : (n + 1) * width] = (total + rsy[n].astype(F32)).astype(BF16)
    for copy in sends:
        copy.wait_send()


def make(sizes):
    ny, nz, nx = sizes
    nh, nj = 2 * nx, 2 * nz
    tok = nh * ROWS
    half = tok // 2
    group = 2 * half
    part = 128 // nz
    width = DOUT // CUTS
    units = 2 * ny + 1

    def body(streams, steps, skip_d, ssm_gain, w_out):
        x = streams.transpose(1, 0, 2)
        dma = pltpu.SemaphoreType.DMA
        scratch = dict(
            kv=pltpu.VMEM((2, 2 * nz, half, 2 * HD), BF16),
            qraw=pltpu.VMEM((tok, 2 * HD), BF16),
            q=pltpu.VMEM((ny, 2, group, HD), BF16),
            feat=pltpu.VMEM((tok, 512), BF16),
            steps_ref=pltpu.VMEM((nh, 4, ROWS), BF16),
            steps_out=pltpu.VMEM((nh, 8, 128), F32),
            steps_in=pltpu.VMEM((nh, 8, 128), F32),
            skip_ref=pltpu.VMEM((1, 2), F32),
            gain_ref=pltpu.VMEM((1, 128), F32),
            w_ref=pltpu.VMEM((3 * HD, DOUT), BF16),
            vt=pltpu.VMEM((2, HD, 4 * half), BF16),
            stat=pltpu.VMEM((8, units * group), F32),
            acc=pltpu.VMEM((HD, units * group), F32),
            pair_out=pltpu.VMEM((2, 128, NST), F32),
            pair_in=pltpu.VMEM((2, 128, NST), F32),
            st_out=pltpu.VMEM((nz, part + 8, NST), F32),
            st_in=pltpu.VMEM((nz, part + 8, NST), F32),
            gt_out=pltpu.VMEM((part + 8, NST), F32),
            gt=pltpu.VMEM((2, ny, part + 8, NST), F32),
            enter=pltpu.VMEM((nz, part, NST), F32),
            reach=pltpu.VMEM((nz, 8, NST), F32),
            carry_out=pltpu.VMEM((nz, part, NST), BF16),
            carry_in=pltpu.VMEM((nz, part, NST), BF16),
            next_out=pltpu.VMEM((128, NST), BF16),
            next_in=pltpu.VMEM((128, NST), BF16),
            o_out=pltpu.VMEM((ny - 1, 2, HD, group), BF16),
            os_out=pltpu.VMEM((ny - 1, 8, group), F32),
            o_in=pltpu.VMEM((ny - 1, 2, HD, group), BF16),
            os_in=pltpu.VMEM((ny - 1, 8, group), F32),
            comb=pltpu.VMEM((tok, 3 * HD), BF16),
            prod=pltpu.VMEM((CUTS, 2, nx, ROWS, width), BF16),
            rsx=pltpu.VMEM((CUTS, nx - 1, 2, ROWS, width), BF16),
            red_out=pltpu.VMEM((CUTS, ROWS, width), BF16),
            rsy=pltpu.VMEM((CUTS, ROWS, width), BF16),
            local_sem=dma((7,)),
            a_send=dma((4, nh)),
            a_recv=dma((4, nh)),
            kv_send=dma((2, nz)),
            kv_recv=dma((2, nz)),
            fw_send=dma((2, nz)),
            fw_recv=dma((2, nz)),
            q_send=dma((ny,)),
            q_recv=dma((ny,)),
            pair_send=dma((2,)),
            pair_recv=dma((2,)),
            st_send=dma((nz,)),
            st_recv=dma((nz,)),
            gt_send=dma((2, ny)),
            gt_recv=dma((2, ny)),
            ca_send=dma((nz,)),
            ca_recv=dma((nz,)),
            o_send=dma((2, ny)),
            o_recv=dma((2, ny)),
            x_send=dma((CUTS, 2, nx)),
            x_recv=dma((CUTS, 2, nx)),
            y_send=dma((CUTS,)),
            y_recv=dma((CUTS,)),
        )
        return pl.pallas_call(
            functools.partial(kernel, sizes),
            out_shape=jax.ShapeDtypeStruct((ROWS, DOUT), BF16),
            in_specs=[pl.BlockSpec(memory_space=pl.ANY)] + [pl.BlockSpec(memory_space=pltpu.HBM)] * 4,
            out_specs=pl.BlockSpec(memory_space=pltpu.VMEM),
            scratch_shapes=list(scratch.values()),
            compiler_params=pltpu.CompilerParams(
                collective_id=0, has_side_effects=True, vmem_limit_bytes=62 * 1024 * 1024
            ),
        )(x, steps.transpose(1, 2, 0), skip_d.reshape(1, 2), ssm_gain.reshape(1, 128), w_out)

    return body


def solution(mesh):
    return jax.shard_map(
        make((N_YLO, N_Z, N_X)),
        mesh=mesh,
        in_specs=(
            P(("ctx", "head"), None, None),
            P(("ctx", "head"), None, None),
            P("head"),
            P("head"),
            P("head", None),
        ),
        out_specs=P(("ctx", "head"), None),
        check_vma=False,
    )
```

```python
import functools
import math

import jax
import jax.numpy as jnp
from jax import lax
from jax.experimental import pallas as pl
from jax.experimental.pallas import tpu as pltpu
from jax.sharding import PartitionSpec as P

HD = 128
HP = 64
NST = 128
ROWS = 16
DOUT = 2560
N_YLO, N_Z, N_CORE, N_YHI, N_X = 4, 8, 2, 2, 4
MESH = pl.DeviceIdType.MESH
F32, BF16 = jnp.float32, jnp.bfloat16
NEG = -1e30
CUTS = 2
TWO_STEPS = False
LEAVE = (0, 4, 2, 1, 3)
PLAN = (
    "keys0",
    "pieces",
    "slices",
    "keys1",
    "queries",
    "pass01",
    "pass02",
    "pass03",
    "pass04",
    "pass05",
    "pass06",
    "pass07",
    "pass11",
    "intra",
    "attend0",
    "pass12",
    "pass13",
    "states",
    "attend1",
    "pass14",
    "pass15",
    "carries",
    "attend2",
    "pass16",
    "pass17",
    "attend3",
)


def nt_dot(a, b):
    return lax.dot_general(a, b, (((1,), (1,)), ((), ())), preferred_element_type=F32)


def nn_dot(a, b):
    return jnp.dot(a, b, preferred_element_type=F32)


def kernel(
    sizes,
    x_hbm,
    steps_hbm,
    skip_hbm,
    gain_hbm,
    w_hbm,
    out_ref,
    x_in_ref,
    x_ref,
    kv,
    qraw,
    q,
    xb,
    zc,
    steps_ref,
    steps_out,
    steps_in,
    skip_ref,
    gain_ref,
    w_ref,
    vt,
    stat,
    acc,
    pair_out,
    pair_in,
    st_out,
    st_in,
    gt_out,
    gt,
    enter,
    reach,
    carry_out,
    carry_in,
    next_out,
    next_in,
    o_out,
    os_out,
    o_in,
    os_in,
    comb,
    prod,
    rsx,
    red_out,
    rsy,
    local_sem,
    a_send,
    a_recv,
    kv_send,
    kv_recv,
    fw_send,
    fw_recv,
    q_send,
    q_recv,
    pair_send,
    pair_recv,
    st_send,
    st_recv,
    gt_send,
    gt_recv,
    ca_send,
    ca_recv,
    o_send,
    o_recv,
    x_send,
    x_recv,
    y_send,
    y_recv,
):
    ny, nz, nx = sizes
    nh, nj = 2 * nx, 2 * nz
    tok = nh * ROWS
    half = tok // 2
    group = 2 * half
    part = 128 // nz
    scale = math.log2(math.e) / math.sqrt(HD)
    order = [0]
    for d in range(1, nz // 2 + 1):
        order += [d] if 2 * d == nz else [d, nz - d]

    c, h = lax.axis_index("ctx"), lax.axis_index("head")
    a, j = c // nj, c % nj
    z, core = j // 2, j % 2
    yh, xx = h // nx, h % nx
    sends = []

    def push(src, dst, send_sem, recv_sem, device):
        copy = pltpu.make_async_remote_copy(
            src_ref=src,
            dst_ref=dst,
            send_sem=send_sem,
            recv_sem=recv_sem,
            device_id=device,
            device_id_type=MESH,
        )
        copy.start()
        sends.append(copy)

    def landed(dst, recv_sem):
        pltpu.make_async_copy(dst, dst, recv_sem).wait()

    def at_ylo(i):
        return (((a + i) % ny) * nj + j, h)

    def at_ylo_other(i):
        return (((a + i) % ny) * nj + z * 2 + (1 - core), h)

    def at_z(d):
        return (a * nj + ((z + d) % nz) * 2 + core, h)

    def at_head(i):
        return (c, (h + i) % nh)

    def at_x(i):
        return (c, yh * nx + (xx + i) % nx)

    sibling = (a * nj + z * 2 + (1 - core), h)
    across = (c, (1 - yh) * nx + xx)

    x_copy = pltpu.make_async_copy(x_hbm, x_in_ref, local_sem.at[8])
    x_copy.start()
    steps_copy = pltpu.make_async_copy(steps_hbm, steps_ref, local_sem.at[4])
    steps_copy.start()
    def rows_of(ref):
        return lambda s: ref.at[pl.ds(pl.multiple_of(s * ROWS, ROWS), ROWS), :]

    places = [
        ((256, 512), lambda s: kv.at[s // nx, 0, pl.ds(pl.multiple_of((s % nx) * ROWS, ROWS), ROWS), :]),
        ((0, 256), rows_of(qraw)),
        ((512, 640, 768, 896), rows_of(xb)),
        ((640, 768, 896, 1024), rows_of(zc)),
    ]
    skip_copy = pltpu.make_async_copy(skip_hbm, skip_ref, local_sem.at[5])
    skip_copy.start()
    gain_copy = pltpu.make_async_copy(gain_hbm, gain_ref, local_sem.at[6])
    gain_copy.start()
    w_copy = pltpu.make_async_copy(w_hbm, w_ref, local_sem.at[7])
    w_copy.start()

    barrier = pltpu.get_barrier_semaphore()
    peers = [at_head(i) for i in range(1, nh)] + [at_z(d) for d in range(1, nz)] + [sibling]
    peers += [at_ylo(i) for i in range(1, ny)] + [at_ylo_other(i) for i in range(1, ny)]
    for peer in peers:
        pl.semaphore_signal(barrier, inc=1, device_id=peer, device_id_type=MESH)

    x_copy.wait()
    own = []
    for n, (cuts, place) in enumerate(places):
        wide = [x_in_ref[:, :, cuts[m] : cuts[m + 1]].astype(F32) for m in range(0, len(cuts), 2)]
        for m, part_of in enumerate(wide):
            at = m * 128
            x_ref[n, :, :, at : at + part_of.shape[2]] = jnp.swapaxes(part_of, 0, 1).astype(BF16)
        copy = pltpu.make_async_copy(x_ref.at[n, h], place(h), local_sem.at[n])
        copy.start()
        own.append(copy)
    pl.semaphore_wait(barrier, len(peers))

    def features_out(n):
        for i in range(1, nh):
            push(x_ref.at[n, (h + i) % nh], places[n][1](h), a_send.at[n, i], a_recv.at[n, i], at_head(i))

    def steps_go():
        steps_copy.wait()
        steps_out[...] = jnp.zeros((nh, 8, 128), F32)
        steps_out[:, 0:4, 0:ROWS] = steps_ref[...].astype(F32)
        for i in range(1, nh):
            push(steps_out.at[(h + i) % nh], steps_in.at[h], a_send.at[4, i], a_recv.at[4, i], at_head(i))
        steps_in[h] = steps_out[h]

    for n in LEAVE:
        if n == 4:
            steps_go()
        else:
            features_out(n)

    def rows_in(n):
        own[n].wait()
        for i in range(1, nh):
            landed(places[n][1]((h + nh - i) % nh), a_recv.at[n, i])

    halves = (yh, 1 - yh)

    def keys(n):
        if n == 0:
            own[0].wait()
        for i in range(n == 0, nx):
            s = halves[n] * nx + (xx + i) % nx
            landed(places[0][1](s), a_recv.at[0, (h + nh - s) % nh])
        mine = kv.at[halves[n], 0]
        for e in range(1, nz):
            if not in_two(order[e]):
                push(mine, kv.at[halves[n], 2 * e], kv_send.at[n, e], kv_recv.at[n, e], at_z(nz - order[e]))
        push(mine, kv.at[halves[n], 1], fw_send.at[n, 0], fw_recv.at[n, 0], sibling)

    def in_two(d):
        return TWO_STEPS and 2 < d < nz - 2

    def onward(block, n, d, by):
        e = order.index(d)
        push(block, kv.at[halves[n], 2 * e], kv_send.at[n, e], kv_recv.at[n, e], at_z(by % nz))

    def pass_on(n, e):
        block = kv.at[halves[n], 2 * e]
        landed(block, kv_recv.at[n, e])
        if order[e] == 2 and in_two(3):
            onward(block, n, 3, -1)
            if n == 0 and in_two(4):
                onward(block, n, 4, -2)
        if order[e] == nz - 2 and in_two(nz - 3):
            onward(block, n, nz - 3, 1)
            if n == 1 and in_two(4):
                onward(block, n, 4, 2)
        push(block, kv.at[halves[n], 2 * e + 1], fw_send.at[n, e], fw_recv.at[n, e], sibling)

    def queries():
        rows_in(1)
        for i in range(2):
            for n in range(2):
                q[0, i, n * half : (n + 1) * half, :] = qraw[i * half : (i + 1) * half, n * HD : (n + 1) * HD]
        for i in range(1, ny):
            push(q.at[0], q.at[ny - i], q_send.at[i], q_recv.at[i], at_ylo(i))

    row_id = lax.broadcasted_iota(jnp.int32, (tok, tok), 0)
    col_id = lax.broadcasted_iota(jnp.int32, (tok, tok), 1)
    same_half = (row_id < half) == (col_id < half)
    lower, upper = (col_id <= row_id) & same_half, (row_id <= col_id) & same_half
    early_row = lax.broadcasted_iota(jnp.int32, (tok, 128), 0) < half
    first_head = lax.broadcasted_iota(jnp.int32, (tok, 128), 1) < HP
    is_early_core = core == 0
    known = {}

    def pieces():
        rows_in(2)
        for i in range(1, nh):
            landed(steps_in.at[(h + nh - i) % nh], a_recv.at[4, i])
        st_t = steps_in[0]
        for g in range(1, nh):
            st_t = st_t + pltpu.roll(steps_in[g], g * ROWS, 1)
        st_t = st_t[:, 0:tok]
        cum_t = nn_dot(st_t.astype(BF16), jnp.where(upper, 1.0, 0.0).astype(BF16))
        total_e, total_l = cum_t[:, half - 1 : half], cum_t[:, tok - 1 : tok]
        early = lax.broadcasted_iota(jnp.int32, (8, tok), 1) < half
        to_end = jnp.exp(jnp.where(early, total_e, total_l) - cum_t)
        x_t = xb[:, 0:128].astype(F32).T
        first_rows = lax.broadcasted_iota(jnp.int32, (128, tok), 0) < HP
        xs_t = x_t * jnp.where(first_rows, to_end[2:3] * st_t[0:1], to_end[3:4] * st_t[1:2])
        b_in = xb[:, 128:256]
        early_lane = lax.broadcasted_iota(jnp.int32, (128, tok), 1) < half
        piece_e = nn_dot(jnp.where(early_lane, xs_t, 0.0).astype(BF16), b_in)
        piece_l = nn_dot(jnp.where(early_lane, 0.0, xs_t).astype(BF16), b_in)
        head_rows = lax.broadcasted_iota(jnp.int32, (128, 128), 0) < HP
        decay_e, decay_l = (
            jnp.exp(jnp.where(head_rows, t[2:3, :], t[3:4, :])) for t in (total_e, total_l)
        )
        pair_out[0] = jnp.where(is_early_core, piece_l, piece_e)
        pair_out[1] = jnp.where(is_early_core, decay_l, decay_e)
        push(pair_out, pair_in, pair_send.at[0], pair_recv.at[0], sibling)
        known["piece"] = jnp.where(is_early_core, piece_e, piece_l)
        known["decay"] = jnp.where(is_early_core, decay_e, decay_l)
        known["cum_t"], known["st_t"] = cum_t, st_t

    def slices():
        landed(pair_in, pair_recv.at[0])
        both = pair_in[1] * known["piece"] + pair_in[0]
        decay = pair_in[1] * known["decay"]
        st_out[:, 0:part, :] = both.reshape(nz, part, NST)
        st_out[:, part:, :] = decay.reshape(nz, part, NST)[:, 0:8, :]
        for d in range(1, nz):
            push(st_out.at[(z + d) % nz], st_in.at[z], st_send.at[d], st_recv.at[d], at_z(d))
        st_in[z] = st_out[z]

    def intra():
        rows_in(3)
        x_in, b_in, c_in = xb[:, 0:128], xb[:, 128:256], zc[:, 128:256]
        cum_t, st_t = known["cum_t"], known["st_t"]
        cum = jnp.concatenate([cum_t, jnp.zeros((120, tok), F32)], axis=0).T
        known["cum"] = cum
        pairs = nt_dot(c_in, b_in)
        within = []
        for s in range(2):
            gap = jnp.where(lower, cum[:, 2 + s : 3 + s] - cum_t[2 + s : 3 + s, :], NEG)
            mix = jnp.exp(gap) * pairs * st_t[s : s + 1, :]
            within.append(nn_dot(mix.astype(BF16), x_in))
        skip_copy.wait()
        skip = jnp.where(first_head, skip_ref[0:1, 0:1], skip_ref[0:1, 1:2])
        known["intra"] = jnp.where(first_head, within[0], within[1]) + skip * x_in.astype(F32)

    key_row = lax.broadcasted_iota(jnp.int32, (4 * half, group), 0)
    q_tok = lax.broadcasted_iota(jnp.int32, (4 * half, group), 1) % half
    picked = [None] + [jnp.where(a + i < ny, 0, 1) for i in range(1, ny)]

    def absorb(scores, values_t, lanes, first):
        top = jnp.max(scores, axis=0, keepdims=True)
        if not first:
            before = stat[0:1, lanes]
            top = jnp.maximum(top, before)
        probs = jnp.exp2(scores * scale - top * scale)
        total = jnp.sum(probs, axis=0, keepdims=True)
        added = nn_dot(values_t, probs.astype(BF16))
        if not first:
            shrink = jnp.exp2((before - top) * scale)
            total = total + stat[1:2, lanes] * shrink
            added = added + acc[:, lanes] * shrink
        stat[0:1, lanes] = top
        stat[1:2, lanes] = total
        acc[:, lanes] = added

    def attend(n):
        first = n == 0
        slots = slice(4 * n, 4 * n + 4)
        for i in range(2):
            vt[i] = kv[i, slots, :, HD : 2 * HD].reshape(4 * half, HD).T
        keys_e = kv[0, slots, :, 0:HD].reshape(4 * half, HD)
        keys_l = kv[1, slots, :, 0:HD].reshape(4 * half, HD)
        absorb(nt_dot(keys_e, q[:, 1].reshape(ny * group, HD)), vt[0], slice(0, ny * group), first)
        for i in range(1, ny):
            s = picked[i]
            at = (ny + i - 1) * group
            keys = kv[s, slots, :, 0:HD].reshape(4 * half, HD)
            absorb(nt_dot(keys, q[i, s]), vt[s], slice(at, at + group), first)
        block = jnp.zeros((4 * half, group), jnp.int32)
        for m in range(4):
            from_z = (z + order[2 * n + m // 2]) % nz
            from_core = core if m % 2 == 0 else 1 - core
            block = jnp.where(key_row // half == m, from_z * 2 + from_core, block)
        key_tok = key_row % half
        see_e = block * half + key_tok <= j * half + q_tok
        see_l = (nj - 1 - block) * half + key_tok <= (nj - 1 - j) * half + q_tok
        at = (2 * ny - 1) * group
        absorb(jnp.where(see_e, nt_dot(keys_e, q[0, 0]), NEG), vt[0], slice(at, at + group), first)
        at = 2 * ny * group
        absorb(jnp.where(see_l, nt_dot(keys_l, q[0, 1]), NEG), vt[1], slice(at, at + group), first)

    def chunk(n):
        if n == 0:
            for i in range(1, ny):
                landed(q.at[ny - i], q_recv.at[i])
        for e in (2 * n, 2 * n + 1):
            for i in range(2):
                landed(kv.at[halves[i], 2 * e + 1], fw_recv.at[i, e])
        attend(n)

    def states_in():
        for d in range(1, nz):
            landed(st_in.at[(z + nz - d) % nz], st_recv.at[d])
        state = jnp.zeros((part, NST), F32)
        decay = jnp.ones((1, NST), F32)
        for k in range(nz):
            at = jnp.where(is_early_core, k, nz - 1 - k)
            enter[at] = state
            reach[at] = jnp.broadcast_to(decay, (8, NST))
            arrived = st_in[at]
            state = arrived[part : part + 1] * state + arrived[0:part]
            decay = arrived[part : part + 1] * decay
        gt_out[0:part, :] = state
        gt_out[part:, :] = jnp.broadcast_to(decay, (8, NST))
        for i in range(1, ny):
            push(gt_out, gt.at[core, a], gt_send.at[0, i], gt_recv.at[0, i], at_ylo(i))
            push(gt_out, gt.at[core, a], gt_send.at[1, i], gt_recv.at[1, i], at_ylo_other(i))
        push(gt_out, gt.at[core, a], gt_send.at[1, 0], gt_recv.at[1, 0], sibling)
        gt[core, a] = gt_out[...]

    def carries_out():
        for i in range(1, ny):
            landed(gt.at[core, (a + ny - i) % ny], gt_recv.at[0, i])
            landed(gt.at[1 - core, (a + ny - i) % ny], gt_recv.at[1, i])
        landed(gt.at[1 - core, a], gt_recv.at[1, 0])
        first = jnp.zeros((part, NST), F32)
        state = jnp.zeros((part, NST), F32)
        for g in range(ny):
            first = jnp.where(is_early_core & (a == g), state, first)
            state = gt[0, g, part : part + 1, :] * state + gt[0, g, 0:part, :]
        for g in reversed(range(ny)):
            first = jnp.where(jnp.logical_not(is_early_core) & (a == g), state, first)
            state = gt[1, g, part : part + 1, :] * state + gt[1, g, 0:part, :]
        for k in range(nz):
            carry_out[k] = (enter[k] + reach[k, 0:1, :] * first).astype(BF16)
        for d in range(1, nz):
            push(carry_out.at[(z + d) % nz], carry_in.at[z], ca_send.at[d], ca_recv.at[d], at_z(d))
        carry_in[z] = carry_out[z]

    def next_state():
        for d in range(1, nz):
            landed(carry_in.at[(z + nz - d) % nz], ca_recv.at[d])
        into = carry_in[...].reshape(128, NST)
        next_out[...] = (known["decay"] * into.astype(F32) + known["piece"]).astype(BF16)
        push(next_out, next_in, pair_send.at[1], pair_recv.at[1], sibling)
        return into

    steps = {"queries": queries, "pieces": pieces, "slices": slices, "intra": intra}
    steps |= {"states": states_in, "carries": carries_out}
    steps |= {f"keys{n}": functools.partial(keys, n) for n in range(2)}
    steps |= {f"pass{n}{e}": functools.partial(pass_on, n, e) for n in range(2) for e in range(1, nz)}
    steps |= {f"attend{n}": functools.partial(chunk, n) for n in range(nz // 2)}
    for name in PLAN:
        if name in steps:
            steps[name]()

    for i in range(1, ny):
        for n, at in enumerate((i * group, (ny + i - 1) * group)):
            o_out[i - 1, n] = acc[:, at : at + group].astype(BF16)
            os_out[i - 1, 2 * n : 2 * n + 2, :] = stat[0:2, at : at + group]
        os_out[i - 1, 4:8, :] = jnp.zeros((4, group), F32)
        push(os_out.at[i - 1], os_in.at[ny - i - 1], o_send.at[0, i], o_recv.at[0, i], at_ylo(i))
        push(o_out.at[i - 1], o_in.at[ny - i - 1], o_send.at[1, i], o_recv.at[1, i], at_ylo(i))

    into = next_state()
    landed(next_in, pair_recv.at[1])
    carry_e = jnp.where(is_early_core, into, next_in[...])
    carry_l = jnp.where(is_early_core, next_in[...], into)
    c_in = zc[:, 128:256]
    inter = jnp.where(early_row, nt_dot(c_in, carry_e), nt_dot(c_in, carry_l))
    cum = known["cum"]
    ssm_y = known["intra"] + inter * jnp.exp(jnp.where(first_head, cum[:, 2:3], cum[:, 3:4]))
    gate = zc[:, 0:128].astype(F32)
    gated = ssm_y * (gate / (1.0 + jnp.exp(-gate)))
    mean_sq = jnp.mean(gated * gated, axis=1, keepdims=True)
    gain_copy.wait()
    comb[:, 2 * HD : 3 * HD] = (gated * lax.rsqrt(mean_sq + 1e-05) * gain_ref[...]).astype(BF16)

    def unit(n):
        lanes = slice(n * group, (n + 1) * group)
        return stat[0:1, lanes], stat[1:2, lanes], acc[:, lanes]

    early, late = [unit(2 * ny - 1)], [unit(0), unit(2 * ny)]
    for i in range(1, ny):
        landed(os_in.at[ny - i - 1], o_recv.at[0, i])
        landed(o_in.at[ny - i - 1], o_recv.at[1, i])
    for i in range(1, ny):
        s = os_in[i - 1]
        late.append((s[0:1], s[1:2], o_in[i - 1, 0].astype(F32)))
        is_early = a + i >= ny
        other = o_in[i - 1, 1].astype(F32)
        early.append((jnp.where(is_early, s[2:3], NEG), s[3:4], other))
        late.append((jnp.where(is_early, NEG, s[2:3]), s[3:4], other))
    for n, parts in enumerate((early, late)):
        top = functools.reduce(jnp.maximum, [p[0] for p in parts])
        total, weighted = 0.0, 0.0
        for m, l, o in parts:
            w = jnp.exp2((m - top) * scale)
            total = total + w * l
            weighted = weighted + w * o
        attn = (weighted / total).T.astype(BF16)
        rows = slice(n * half, (n + 1) * half)
        comb[rows, 0:HD] = attn[0:half]
        comb[rows, HD : 2 * HD] = attn[half:]

    w_copy.wait()
    width = DOUT // CUTS

    def over_x(n, way):
        for i in range(1, nx):
            push(
                prod.at[n, halves[1 - way], (xx + i) % nx],
                rsx.at[n, nx - i - 1, way],
                x_send.at[n, way, i],
                x_recv.at[n, way, i],
                at_x(i),
            )

    def sum_over_x(n, way):
        for i in range(1, nx):
            landed(rsx.at[n, nx - i - 1, way], x_recv.at[n, way, i])
        total = prod[n, halves[1 - way], xx].astype(F32)
        for i in range(nx - 1):
            total = total + rsx[n, i, way].astype(F32)
        return total

    def project(n, way):
        rows = pl.ds(pl.multiple_of(halves[1 - way] * half, half), half)
        share = nn_dot(comb[rows, :], w_ref[:, n * width : (n + 1) * width]).astype(BF16)
        prod[n, halves[1 - way]] = share.reshape(nx, ROWS, width)

    for n in range(CUTS):
        project(n, 0)
        over_x(n, 0)
    for n in range(CUTS):
        project(n, 1)
    for n in range(CUTS):
        red_out[n] = sum_over_x(n, 0).astype(BF16)
        push(red_out.at[n], rsy.at[n], y_send.at[n], y_recv.at[n], across)
        over_x(n, 1)
    for n in range(CUTS):
        total = sum_over_x(n, 1)
        landed(rsy.at[n], y_recv.at[n])
        out_ref[:, n * width : (n + 1) * width] = (total + rsy[n].astype(F32)).astype(BF16)
    for copy in sends:
        copy.wait_send()


def make(sizes):
    ny, nz, nx = sizes
    nh, nj = 2 * nx, 2 * nz
    tok = nh * ROWS
    half = tok // 2
    group = 2 * half
    part = 128 // nz
    width = DOUT // CUTS
    units = 2 * ny + 1

    def body(streams, steps, skip_d, ssm_gain, w_out):
        dma = pltpu.SemaphoreType.DMA
        scratch = dict(
            x_in_ref=pltpu.VMEM((ROWS, nh, 1024), BF16),
            x_ref=pltpu.VMEM((4, nh, ROWS, 256), BF16),
            kv=pltpu.VMEM((2, 2 * nz, half, 2 * HD), BF16),
            qraw=pltpu.VMEM((tok, 2 * HD), BF16),
            q=pltpu.VMEM((ny, 2, group, HD), BF16),
            xb=pltpu.VMEM((tok, 256), BF16),
            zc=pltpu.VMEM((tok, 256), BF16),
            steps_ref=pltpu.VMEM((nh, 4, ROWS), BF16),
            steps_out=pltpu.VMEM((nh, 8, 128), F32),
            steps_in=pltpu.VMEM((nh, 8, 128), F32),
            skip_ref=pltpu.VMEM((1, 2), F32),
            gain_ref=pltpu.VMEM((1, 128), F32),
            w_ref=pltpu.VMEM((3 * HD, DOUT), BF16),
            vt=pltpu.VMEM((2, HD, 4 * half), BF16),
            stat=pltpu.VMEM((8, units * group), F32),
            acc=pltpu.VMEM((HD, units * group), F32),
            pair_out=pltpu.VMEM((2, 128, NST), F32),
            pair_in=pltpu.VMEM((2, 128, NST), F32),
            st_out=pltpu.VMEM((nz, part + 8, NST), F32),
            st_in=pltpu.VMEM((nz, part + 8, NST), F32),
            gt_out=pltpu.VMEM((part + 8, NST), F32),
            gt=pltpu.VMEM((2, ny, part + 8, NST), F32),
            enter=pltpu.VMEM((nz, part, NST), F32),
            reach=pltpu.VMEM((nz, 8, NST), F32),
            carry_out=pltpu.VMEM((nz, part, NST), BF16),
            carry_in=pltpu.VMEM((nz, part, NST), BF16),
            next_out=pltpu.VMEM((128, NST), BF16),
            next_in=pltpu.VMEM((128, NST), BF16),
            o_out=pltpu.VMEM((ny - 1, 2, HD, group), BF16),
            os_out=pltpu.VMEM((ny - 1, 8, group), F32),
            o_in=pltpu.VMEM((ny - 1, 2, HD, group), BF16),
            os_in=pltpu.VMEM((ny - 1, 8, group), F32),
            comb=pltpu.VMEM((tok, 3 * HD), BF16),
            prod=pltpu.VMEM((CUTS, 2, nx, ROWS, width), BF16),
            rsx=pltpu.VMEM((CUTS, nx - 1, 2, ROWS, width), BF16),
            red_out=pltpu.VMEM((CUTS, ROWS, width), BF16),
            rsy=pltpu.VMEM((CUTS, ROWS, width), BF16),
            local_sem=dma((9,)),
            a_send=dma((5, nh)),
            a_recv=dma((5, nh)),
            kv_send=dma((2, nz)),
            kv_recv=dma((2, nz)),
            fw_send=dma((2, nz)),
            fw_recv=dma((2, nz)),
            q_send=dma((ny,)),
            q_recv=dma((ny,)),
            pair_send=dma((2,)),
            pair_recv=dma((2,)),
            st_send=dma((nz,)),
            st_recv=dma((nz,)),
            gt_send=dma((2, ny)),
            gt_recv=dma((2, ny)),
            ca_send=dma((nz,)),
            ca_recv=dma((nz,)),
            o_send=dma((2, ny)),
            o_recv=dma((2, ny)),
            x_send=dma((CUTS, 2, nx)),
            x_recv=dma((CUTS, 2, nx)),
            y_send=dma((CUTS,)),
            y_recv=dma((CUTS,)),
        )
        return pl.pallas_call(
            functools.partial(kernel, sizes),
            out_shape=jax.ShapeDtypeStruct((ROWS, DOUT), BF16),
            in_specs=[pl.BlockSpec(memory_space=pl.ANY)] + [pl.BlockSpec(memory_space=pltpu.HBM)] * 4,
            out_specs=pl.BlockSpec(memory_space=pltpu.VMEM),
            scratch_shapes=list(scratch.values()),
            compiler_params=pltpu.CompilerParams(
                collective_id=0, has_side_effects=True, vmem_limit_bytes=62 * 1024 * 1024
            ),
        )(streams, steps.transpose(1, 2, 0), skip_d.reshape(1, 2), ssm_gain.reshape(1, 128), w_out)

    return body


def solution(mesh):
    return jax.shard_map(
        make((N_YLO, N_Z, N_X)),
        mesh=mesh,
        in_specs=(
            P(("ctx", "head"), None, None),
            P(("ctx", "head"), None, None),
            P("head"),
            P("head"),
            P("head", None),
        ),
        out_specs=P(("ctx", "head"), None),
        check_vma=False,
    )
```

```python
import functools
import math

import jax
import jax.numpy as jnp
from jax import lax
from jax.experimental import pallas as pl
from jax.experimental.pallas import tpu as pltpu
from jax.sharding import PartitionSpec as P

HD = 128
HP = 64
NST = 128
ROWS = 16
DOUT = 2560
N_YLO, N_Z, N_CORE, N_YHI, N_X = 4, 8, 2, 2, 4
MESH = pl.DeviceIdType.MESH
F32, BF16 = jnp.float32, jnp.bfloat16
NEG = -1e30
CUTS = 2
TWO_STEPS = False
LEAVE = (0, 4, 2, 1, 3)
PLAN = (
    "keys0",
    "pieces",
    "slices",
    "keys1",
    "queries",
    "pass01",
    "pass02",
    "pass03",
    "pass04",
    "pass05",
    "pass06",
    "pass07",
    "pass11",
    "intra",
    "attend0",
    "pass12",
    "pass13",
    "states",
    "attend1",
    "pass14",
    "pass15",
    "pass16",
    "pass17",
    "attend2",
    "carries",
    "attend3",
)


def nt_dot(a, b):
    return lax.dot_general(a, b, (((1,), (1,)), ((), ())), preferred_element_type=F32)


def nn_dot(a, b):
    return jnp.dot(a, b, preferred_element_type=F32)


def kernel(
    sizes,
    x_hbm,
    steps_hbm,
    skip_hbm,
    gain_hbm,
    w_hbm,
    out_ref,
    x_in_ref,
    x_ref,
    kv,
    qraw,
    q,
    xb,
    zc,
    steps_ref,
    steps_out,
    steps_in,
    skip_ref,
    gain_ref,
    w_ref,
    vt,
    stat,
    acc,
    pair_out,
    pair_in,
    st_out,
    st_in,
    gt_out,
    gt,
    enter,
    reach,
    carry_out,
    carry_in,
    next_out,
    next_in,
    o_out,
    os_out,
    o_in,
    os_in,
    comb,
    prod,
    rsx,
    red_out,
    rsy,
    local_sem,
    a_send,
    a_recv,
    kv_send,
    kv_recv,
    fw_send,
    fw_recv,
    q_send,
    q_recv,
    pair_send,
    pair_recv,
    st_send,
    st_recv,
    gt_send,
    gt_recv,
    ca_send,
    ca_recv,
    o_send,
    o_recv,
    x_send,
    x_recv,
    y_send,
    y_recv,
):
    ny, nz, nx = sizes
    nh, nj = 2 * nx, 2 * nz
    tok = nh * ROWS
    half = tok // 2
    group = 2 * half
    part = 128 // nz
    scale = math.log2(math.e) / math.sqrt(HD)
    order = [0]
    for d in range(1, nz // 2 + 1):
        order += [d] if 2 * d == nz else [d, nz - d]

    c, h = lax.axis_index("ctx"), lax.axis_index("head")
    a, j = c // nj, c % nj
    z, core = j // 2, j % 2
    yh, xx = h // nx, h % nx
    sends = []

    def push(src, dst, send_sem, recv_sem, device):
        copy = pltpu.make_async_remote_copy(
            src_ref=src,
            dst_ref=dst,
            send_sem=send_sem,
            recv_sem=recv_sem,
            device_id=device,
            device_id_type=MESH,
        )
        copy.start()
        sends.append(copy)

    def landed(dst, recv_sem):
        pltpu.make_async_copy(dst, dst, recv_sem).wait()

    def at_ylo(i):
        return (((a + i) % ny) * nj + j, h)

    def at_ylo_other(i):
        return (((a + i) % ny) * nj + z * 2 + (1 - core), h)

    def at_z(d):
        return (a * nj + ((z + d) % nz) * 2 + core, h)

    def at_head(i):
        return (c, (h + i) % nh)

    def at_x(i):
        return (c, yh * nx + (xx + i) % nx)

    sibling = (a * nj + z * 2 + (1 - core), h)
    across = (c, (1 - yh) * nx + xx)

    x_copy = pltpu.make_async_copy(x_hbm, x_in_ref, local_sem.at[8])
    x_copy.start()
    steps_copy = pltpu.make_async_copy(steps_hbm, steps_ref, local_sem.at[4])
    steps_copy.start()
    def rows_of(ref):
        return lambda s: ref.at[pl.ds(pl.multiple_of(s * ROWS, ROWS), ROWS), :]

    places = [
        ((256, 512), lambda s: kv.at[s // nx, 0, pl.ds(pl.multiple_of((s % nx) * ROWS, ROWS), ROWS), :]),
        ((0, 256), rows_of(qraw)),
        ((512, 640, 768, 896), rows_of(xb)),
        ((640, 768, 896, 1024), rows_of(zc)),
    ]
    skip_copy = pltpu.make_async_copy(skip_hbm, skip_ref, local_sem.at[5])
    skip_copy.start()
    gain_copy = pltpu.make_async_copy(gain_hbm, gain_ref, local_sem.at[6])
    gain_copy.start()
    w_copy = pltpu.make_async_copy(w_hbm, w_ref, local_sem.at[7])
    w_copy.start()

    barrier = pltpu.get_barrier_semaphore()
    peers = [at_head(i) for i in range(1, nh)] + [at_z(d) for d in range(1, nz)] + [sibling]
    peers += [at_ylo(i) for i in range(1, ny)] + [at_ylo_other(i) for i in range(1, ny)]
    for peer in peers:
        pl.semaphore_signal(barrier, inc=1, device_id=peer, device_id_type=MESH)

    x_copy.wait()
    own = []
    for n, (cuts, place) in enumerate(places):
        wide = [x_in_ref[:, :, cuts[m] : cuts[m + 1]].astype(F32) for m in range(0, len(cuts), 2)]
        for m, part_of in enumerate(wide):
            at = m * 128
            x_ref[n, :, :, at : at + part_of.shape[2]] = jnp.swapaxes(part_of, 0, 1).astype(BF16)
        copy = pltpu.make_async_copy(x_ref.at[n, h], place(h), local_sem.at[n])
        copy.start()
        own.append(copy)
    pl.semaphore_wait(barrier, len(peers))

    def features_out(n):
        for i in range(1, nh):
            push(x_ref.at[n, (h + i) % nh], places[n][1](h), a_send.at[n, i], a_recv.at[n, i], at_head(i))

    def steps_go():
        steps_copy.wait()
        steps_out[...] = jnp.zeros((nh, 8, 128), F32)
        steps_out[:, 0:4, 0:ROWS] = steps_ref[...].astype(F32)
        for i in range(1, nh):
            push(steps_out.at[(h + i) % nh], steps_in.at[h], a_send.at[4, i], a_recv.at[4, i], at_head(i))
        steps_in[h] = steps_out[h]

    for n in LEAVE:
        if n == 4:
            steps_go()
        else:
            features_out(n)

    def rows_in(n):
        own[n].wait()
        for i in range(1, nh):
            landed(places[n][1]((h + nh - i) % nh), a_recv.at[n, i])

    halves = (yh, 1 - yh)

    def keys(n):
        if n == 0:
            own[0].wait()
        for i in range(n == 0, nx):
            s = halves[n] * nx + (xx + i) % nx
            landed(places[0][1](s), a_recv.at[0, (h + nh - s) % nh])
        mine = kv.at[halves[n], 0]
        for e in range(1, nz):
            if not in_two(order[e]):
                push(mine, kv.at[halves[n], 2 * e], kv_send.at[n, e], kv_recv.at[n, e], at_z(nz - order[e]))
        push(mine, kv.at[halves[n], 1], fw_send.at[n, 0], fw_recv.at[n, 0], sibling)

    def in_two(d):
        return TWO_STEPS and 2 < d < nz - 2

    def onward(block, n, d, by):
        e = order.index(d)
        push(block, kv.at[halves[n], 2 * e], kv_send.at[n, e], kv_recv.at[n, e], at_z(by % nz))

    def pass_on(n, e):
        block = kv.at[halves[n], 2 * e]
        landed(block, kv_recv.at[n, e])
        if order[e] == 2 and in_two(3):
            onward(block, n, 3, -1)
            if n == 0 and in_two(4):
                onward(block, n, 4, -2)
        if order[e] == nz - 2 and in_two(nz - 3):
            onward(block, n, nz - 3, 1)
            if n == 1 and in_two(4):
                onward(block, n, 4, 2)
        push(block, kv.at[halves[n], 2 * e + 1], fw_send.at[n, e], fw_recv.at[n, e], sibling)

    def queries():
        rows_in(1)
        for i in range(2):
            for n in range(2):
                q[0, i, n * half : (n + 1) * half, :] = qraw[i * half : (i + 1) * half, n * HD : (n + 1) * HD]
        for i in range(1, ny):
            push(q.at[0], q.at[ny - i], q_send.at[i], q_recv.at[i], at_ylo(i))

    row_id = lax.broadcasted_iota(jnp.int32, (tok, tok), 0)
    col_id = lax.broadcasted_iota(jnp.int32, (tok, tok), 1)
    same_half = (row_id < half) == (col_id < half)
    lower, upper = (col_id <= row_id) & same_half, (row_id <= col_id) & same_half
    early_row = lax.broadcasted_iota(jnp.int32, (tok, 128), 0) < half
    first_head = lax.broadcasted_iota(jnp.int32, (tok, 128), 1) < HP
    is_early_core = core == 0
    known = {}

    def pieces():
        rows_in(2)
        for i in range(1, nh):
            landed(steps_in.at[(h + nh - i) % nh], a_recv.at[4, i])
        st_t = steps_in[0]
        for g in range(1, nh):
            st_t = st_t + pltpu.roll(steps_in[g], g * ROWS, 1)
        st_t = st_t[:, 0:tok]
        cum_t = nn_dot(st_t.astype(BF16), jnp.where(upper, 1.0, 0.0).astype(BF16))
        total_e, total_l = cum_t[:, half - 1 : half], cum_t[:, tok - 1 : tok]
        early = lax.broadcasted_iota(jnp.int32, (8, tok), 1) < half
        to_end = jnp.exp(jnp.where(early, total_e, total_l) - cum_t)
        x_t = xb[:, 0:128].astype(F32).T
        first_rows = lax.broadcasted_iota(jnp.int32, (128, tok), 0) < HP
        xs_t = x_t * jnp.where(first_rows, to_end[2:3] * st_t[0:1], to_end[3:4] * st_t[1:2])
        b_in = xb[:, 128:256]
        early_lane = lax.broadcasted_iota(jnp.int32, (128, tok), 1) < half
        piece_e = nn_dot(jnp.where(early_lane, xs_t, 0.0).astype(BF16), b_in)
        piece_l = nn_dot(jnp.where(early_lane, 0.0, xs_t).astype(BF16), b_in)
        head_rows = lax.broadcasted_iota(jnp.int32, (128, 128), 0) < HP
        decay_e, decay_l = (
            jnp.exp(jnp.where(head_rows, t[2:3, :], t[3:4, :])) for t in (total_e, total_l)
        )
        pair_out[0] = jnp.where(is_early_core, piece_l, piece_e)
        pair_out[1] = jnp.where(is_early_core, decay_l, decay_e)
        push(pair_out, pair_in, pair_send.at[0], pair_recv.at[0], sibling)
        known["piece"] = jnp.where(is_early_core, piece_e, piece_l)
        known["decay"] = jnp.where(is_early_core, decay_e, decay_l)
        known["cum_t"], known["st_t"] = cum_t, st_t

    def slices():
        landed(pair_in, pair_recv.at[0])
        both = pair_in[1] * known["piece"] + pair_in[0]
        decay = pair_in[1] * known["decay"]
        st_out[:, 0:part, :] = both.reshape(nz, part, NST)
        st_out[:, part:, :] = decay.reshape(nz, part, NST)[:, 0:8, :]
        for d in range(1, nz):
            push(st_out.at[(z + d) % nz], st_in.at[z], st_send.at[d], st_recv.at[d], at_z(d))
        st_in[z] = st_out[z]

    def intra():
        rows_in(3)
        x_in, b_in, c_in = xb[:, 0:128], xb[:, 128:256], zc[:, 128:256]
        cum_t, st_t = known["cum_t"], known["st_t"]
        cum = jnp.concatenate([cum_t, jnp.zeros((120, tok), F32)], axis=0).T
        pairs = nt_dot(c_in, b_in)
        within = []
        for s in range(2):
            gap = jnp.where(lower, cum[:, 2 + s : 3 + s] - cum_t[2 + s : 3 + s, :], NEG)
            mix = jnp.exp(gap) * pairs * st_t[s : s + 1, :]
            within.append(nn_dot(mix.astype(BF16), x_in))
        skip_copy.wait()
        skip = jnp.where(first_head, skip_ref[0:1, 0:1], skip_ref[0:1, 1:2])
        gate = zc[:, 0:128].astype(F32)
        gate = gate / (1.0 + jnp.exp(-gate))
        known["intra"] = (jnp.where(first_head, within[0], within[1]) + skip * x_in.astype(F32)) * gate
        known["gain"] = jnp.exp(jnp.where(first_head, cum[:, 2:3], cum[:, 3:4])) * gate

    key_row = lax.broadcasted_iota(jnp.int32, (4 * half, group), 0)
    q_tok = lax.broadcasted_iota(jnp.int32, (4 * half, group), 1) % half
    picked = [None] + [jnp.where(a + i < ny, 0, 1) for i in range(1, ny)]

    def absorb(scores, values_t, lanes, first):
        top = jnp.max(scores, axis=0, keepdims=True)
        if not first:
            before = stat[0:1, lanes]
            top = jnp.maximum(top, before)
        probs = jnp.exp2(scores * scale - top * scale)
        total = jnp.sum(probs, axis=0, keepdims=True)
        added = nn_dot(values_t, probs.astype(BF16))
        if not first:
            shrink = jnp.exp2((before - top) * scale)
            total = total + stat[1:2, lanes] * shrink
            added = added + acc[:, lanes] * shrink
        stat[0:1, lanes] = top
        stat[1:2, lanes] = total
        acc[:, lanes] = added

    def attend(n):
        first = n == 0
        slots = slice(4 * n, 4 * n + 4)
        for i in range(2):
            vt[i] = kv[i, slots, :, HD : 2 * HD].reshape(4 * half, HD).T
        keys_e = kv[0, slots, :, 0:HD].reshape(4 * half, HD)
        keys_l = kv[1, slots, :, 0:HD].reshape(4 * half, HD)
        absorb(nt_dot(keys_e, q[:, 1].reshape(ny * group, HD)), vt[0], slice(0, ny * group), first)
        for i in range(1, ny):
            s = picked[i]
            at = (ny + i - 1) * group
            keys = kv[s, slots, :, 0:HD].reshape(4 * half, HD)
            absorb(nt_dot(keys, q[i, s]), vt[s], slice(at, at + group), first)
        block = jnp.zeros((4 * half, group), jnp.int32)
        for m in range(4):
            from_z = (z + order[2 * n + m // 2]) % nz
            from_core = core if m % 2 == 0 else 1 - core
            block = jnp.where(key_row // half == m, from_z * 2 + from_core, block)
        key_tok = key_row % half
        see_e = block * half + key_tok <= j * half + q_tok
        see_l = (nj - 1 - block) * half + key_tok <= (nj - 1 - j) * half + q_tok
        at = (2 * ny - 1) * group
        absorb(jnp.where(see_e, nt_dot(keys_e, q[0, 0]), NEG), vt[0], slice(at, at + group), first)
        at = 2 * ny * group
        absorb(jnp.where(see_l, nt_dot(keys_l, q[0, 1]), NEG), vt[1], slice(at, at + group), first)

    def chunk(n):
        if n == 0:
            for i in range(1, ny):
                landed(q.at[ny - i], q_recv.at[i])
        for e in (2 * n, 2 * n + 1):
            for i in range(2):
                landed(kv.at[halves[i], 2 * e + 1], fw_recv.at[i, e])
        attend(n)

    def states_in():
        for d in range(1, nz):
            landed(st_in.at[(z + nz - d) % nz], st_recv.at[d])
        state = jnp.zeros((part, NST), F32)
        decay = jnp.ones((1, NST), F32)
        for k in range(nz):
            at = jnp.where(is_early_core, k, nz - 1 - k)
            enter[at] = state
            reach[at] = jnp.broadcast_to(decay, (8, NST))
            arrived = st_in[at]
            state = arrived[part : part + 1] * state + arrived[0:part]
            decay = arrived[part : part + 1] * decay
        gt_out[0:part, :] = state
        gt_out[part:, :] = jnp.broadcast_to(decay, (8, NST))
        for i in range(1, ny):
            push(gt_out, gt.at[core, a], gt_send.at[0, i], gt_recv.at[0, i], at_ylo(i))
            push(gt_out, gt.at[core, a], gt_send.at[1, i], gt_recv.at[1, i], at_ylo_other(i))
        push(gt_out, gt.at[core, a], gt_send.at[1, 0], gt_recv.at[1, 0], sibling)
        gt[core, a] = gt_out[...]

    def carries_out():
        for i in range(1, ny):
            landed(gt.at[core, (a + ny - i) % ny], gt_recv.at[0, i])
            landed(gt.at[1 - core, (a + ny - i) % ny], gt_recv.at[1, i])
        landed(gt.at[1 - core, a], gt_recv.at[1, 0])
        first = jnp.zeros((part, NST), F32)
        state = jnp.zeros((part, NST), F32)
        for g in range(ny):
            first = jnp.where(is_early_core & (a == g), state, first)
            state = gt[0, g, part : part + 1, :] * state + gt[0, g, 0:part, :]
        for g in reversed(range(ny)):
            first = jnp.where(jnp.logical_not(is_early_core) & (a == g), state, first)
            state = gt[1, g, part : part + 1, :] * state + gt[1, g, 0:part, :]
        for k in range(nz):
            carry_out[k] = (enter[k] + reach[k, 0:1, :] * first).astype(BF16)
        for d in range(1, nz):
            push(carry_out.at[(z + d) % nz], carry_in.at[z], ca_send.at[d], ca_recv.at[d], at_z(d))
        carry_in[z] = carry_out[z]

    def next_state():
        for d in range(1, nz):
            landed(carry_in.at[(z + nz - d) % nz], ca_recv.at[d])
        into = carry_in[...].reshape(128, NST)
        next_out[...] = (known["decay"] * into.astype(F32) + known["piece"]).astype(BF16)
        push(next_out, next_in, pair_send.at[1], pair_recv.at[1], sibling)
        return into

    steps = {"queries": queries, "pieces": pieces, "slices": slices, "intra": intra}
    steps |= {"states": states_in, "carries": carries_out}
    steps |= {f"keys{n}": functools.partial(keys, n) for n in range(2)}
    steps |= {f"pass{n}{e}": functools.partial(pass_on, n, e) for n in range(2) for e in range(1, nz)}
    steps |= {f"attend{n}": functools.partial(chunk, n) for n in range(nz // 2)}
    for name in PLAN:
        if name in steps:
            steps[name]()

    for i in range(1, ny):
        for n, at in enumerate((i * group, (ny + i - 1) * group)):
            o_out[i - 1, n] = acc[:, at : at + group].astype(BF16)
            os_out[i - 1, 2 * n : 2 * n + 2, :] = stat[0:2, at : at + group]
        os_out[i - 1, 4:8, :] = jnp.zeros((4, group), F32)
        push(os_out.at[i - 1], os_in.at[ny - i - 1], o_send.at[0, i], o_recv.at[0, i], at_ylo(i))
        push(o_out.at[i - 1], o_in.at[ny - i - 1], o_send.at[1, i], o_recv.at[1, i], at_ylo(i))

    into = next_state()
    c_in = zc[:, 128:256]
    by_own = nt_dot(c_in, into)
    landed(next_in, pair_recv.at[1])
    inter = jnp.where(early_row == is_early_core, by_own, nt_dot(c_in, next_in[...]))
    gated = known["intra"] + inter * known["gain"]
    mean_sq = jnp.mean(gated * gated, axis=1, keepdims=True)
    gain_copy.wait()
    comb[:, 2 * HD : 3 * HD] = (gated * lax.rsqrt(mean_sq + 1e-05) * gain_ref[...]).astype(BF16)

    def unit(n):
        lanes = slice(n * group, (n + 1) * group)
        return stat[0:1, lanes], stat[1:2, lanes], acc[:, lanes]

    early, late = [unit(2 * ny - 1)], [unit(0), unit(2 * ny)]
    for i in range(1, ny):
        landed(os_in.at[ny - i - 1], o_recv.at[0, i])
        landed(o_in.at[ny - i - 1], o_recv.at[1, i])
    for i in range(1, ny):
        s = os_in[i - 1]
        late.append((s[0:1], s[1:2], o_in[i - 1, 0].astype(F32)))
        is_early = a + i >= ny
        other = o_in[i - 1, 1].astype(F32)
        early.append((jnp.where(is_early, s[2:3], NEG), s[3:4], other))
        late.append((jnp.where(is_early, NEG, s[2:3]), s[3:4], other))
    for n, parts in enumerate((early, late)):
        top = functools.reduce(jnp.maximum, [p[0] for p in parts])
        total, weighted = 0.0, 0.0
        for m, l, o in parts:
            w = jnp.exp2((m - top) * scale)
            total = total + w * l
            weighted = weighted + w * o
        attn = (weighted / total).T.astype(BF16)
        rows = slice(n * half, (n + 1) * half)
        comb[rows, 0:HD] = attn[0:half]
        comb[rows, HD : 2 * HD] = attn[half:]

    w_copy.wait()
    width = DOUT // CUTS

    def over_x(n, way):
        for i in range(1, nx):
            push(
                prod.at[n, halves[1 - way], (xx + i) % nx],
                rsx.at[n, nx - i - 1, way],
                x_send.at[n, way, i],
                x_recv.at[n, way, i],
                at_x(i),
            )

    def sum_over_x(n, way):
        for i in range(1, nx):
            landed(rsx.at[n, nx - i - 1, way], x_recv.at[n, way, i])
        total = prod[n, halves[1 - way], xx].astype(F32)
        for i in range(nx - 1):
            total = total + rsx[n, i, way].astype(F32)
        return total

    def project(n, way):
        rows = pl.ds(pl.multiple_of(halves[1 - way] * half, half), half)
        share = nn_dot(comb[rows, :], w_ref[:, n * width : (n + 1) * width]).astype(BF16)
        prod[n, halves[1 - way]] = share.reshape(nx, ROWS, width)

    for n in range(CUTS):
        project(n, 0)
        over_x(n, 0)
    for n in range(CUTS):
        project(n, 1)
    for n in range(CUTS):
        red_out[n] = sum_over_x(n, 0).astype(BF16)
        push(red_out.at[n], rsy.at[n], y_send.at[n], y_recv.at[n], across)
        over_x(n, 1)
    for n in range(CUTS):
        total = sum_over_x(n, 1)
        landed(rsy.at[n], y_recv.at[n])
        out_ref[:, n * width : (n + 1) * width] = (total + rsy[n].astype(F32)).astype(BF16)
    for copy in sends:
        copy.wait_send()


def make(sizes):
    ny, nz, nx = sizes
    nh, nj = 2 * nx, 2 * nz
    tok = nh * ROWS
    half = tok // 2
    group = 2 * half
    part = 128 // nz
    width = DOUT // CUTS
    units = 2 * ny + 1

    def body(streams, steps, skip_d, ssm_gain, w_out):
        dma = pltpu.SemaphoreType.DMA
        scratch = dict(
            x_in_ref=pltpu.VMEM((ROWS, nh, 1024), BF16),
            x_ref=pltpu.VMEM((4, nh, ROWS, 256), BF16),
            kv=pltpu.VMEM((2, 2 * nz, half, 2 * HD), BF16),
            qraw=pltpu.VMEM((tok, 2 * HD), BF16),
            q=pltpu.VMEM((ny, 2, group, HD), BF16),
            xb=pltpu.VMEM((tok, 256), BF16),
            zc=pltpu.VMEM((tok, 256), BF16),
            steps_ref=pltpu.VMEM((nh, 4, ROWS), BF16),
            steps_out=pltpu.VMEM((nh, 8, 128), F32),
            steps_in=pltpu.VMEM((nh, 8, 128), F32),
            skip_ref=pltpu.VMEM((1, 2), F32),
            gain_ref=pltpu.VMEM((1, 128), F32),
            w_ref=pltpu.VMEM((3 * HD, DOUT), BF16),
            vt=pltpu.VMEM((2, HD, 4 * half), BF16),
            stat=pltpu.VMEM((8, units * group), F32),
            acc=pltpu.VMEM((HD, units * group), F32),
            pair_out=pltpu.VMEM((2, 128, NST), F32),
            pair_in=pltpu.VMEM((2, 128, NST), F32),
            st_out=pltpu.VMEM((nz, part + 8, NST), F32),
            st_in=pltpu.VMEM((nz, part + 8, NST), F32),
            gt_out=pltpu.VMEM((part + 8, NST), F32),
            gt=pltpu.VMEM((2, ny, part + 8, NST), F32),
            enter=pltpu.VMEM((nz, part, NST), F32),
            reach=pltpu.VMEM((nz, 8, NST), F32),
            carry_out=pltpu.VMEM((nz, part, NST), BF16),
            carry_in=pltpu.VMEM((nz, part, NST), BF16),
            next_out=pltpu.VMEM((128, NST), BF16),
            next_in=pltpu.VMEM((128, NST), BF16),
            o_out=pltpu.VMEM((ny - 1, 2, HD, group), BF16),
            os_out=pltpu.VMEM((ny - 1, 8, group), F32),
            o_in=pltpu.VMEM((ny - 1, 2, HD, group), BF16),
            os_in=pltpu.VMEM((ny - 1, 8, group), F32),
            comb=pltpu.VMEM((tok, 3 * HD), BF16),
            prod=pltpu.VMEM((CUTS, 2, nx, ROWS, width), BF16),
            rsx=pltpu.VMEM((CUTS, nx - 1, 2, ROWS, width), BF16),
            red_out=pltpu.VMEM((CUTS, ROWS, width), BF16),
            rsy=pltpu.VMEM((CUTS, ROWS, width), BF16),
            local_sem=dma((9,)),
            a_send=dma((5, nh)),
            a_recv=dma((5, nh)),
            kv_send=dma((2, nz)),
            kv_recv=dma((2, nz)),
            fw_send=dma((2, nz)),
            fw_recv=dma((2, nz)),
            q_send=dma((ny,)),
            q_recv=dma((ny,)),
            pair_send=dma((2,)),
            pair_recv=dma((2,)),
            st_send=dma((nz,)),
            st_recv=dma((nz,)),
            gt_send=dma((2, ny)),
            gt_recv=dma((2, ny)),
            ca_send=dma((nz,)),
            ca_recv=dma((nz,)),
            o_send=dma((2, ny)),
            o_recv=dma((2, ny)),
            x_send=dma((CUTS, 2, nx)),
            x_recv=dma((CUTS, 2, nx)),
            y_send=dma((CUTS,)),
            y_recv=dma((CUTS,)),
        )
        return pl.pallas_call(
            functools.partial(kernel, sizes),
            out_shape=jax.ShapeDtypeStruct((ROWS, DOUT), BF16),
            in_specs=[pl.BlockSpec(memory_space=pl.ANY)] + [pl.BlockSpec(memory_space=pltpu.HBM)] * 4,
            out_specs=pl.BlockSpec(memory_space=pltpu.VMEM),
            scratch_shapes=list(scratch.values()),
            compiler_params=pltpu.CompilerParams(
                collective_id=0, has_side_effects=True, vmem_limit_bytes=62 * 1024 * 1024
            ),
        )(streams, steps.transpose(1, 2, 0), skip_d.reshape(1, 2), ssm_gain.reshape(1, 128), w_out)

    return body


def solution(mesh):
    return jax.shard_map(
        make((N_YLO, N_Z, N_X)),
        mesh=mesh,
        in_specs=(
            P(("ctx", "head"), None, None),
            P(("ctx", "head"), None, None),
            P("head"),
            P("head"),
            P("head", None),
        ),
        out_specs=P(("ctx", "head"), None),
        check_vma=False,
    )
```
